128 devices in a mesh: layer: 2 (over core), gy: 8 (over y_lo, z), gx: 8 (over x, y_hi).
Axes of the slice: x: 4, y: 4 (y_hi: 2, y_lo: 2; y = y_hi * 2 + y_lo), z: 4, core: 2. Of those that a mesh axis runs over, the one named last changes fastest.
Arguments:
- frames: bfloat16 [2, 32, 2048, 256], P(None, 'gy', 'gx'), may hold values from -6 to 6
- hidden_init: bfloat16 [2, 32, 2048, 256], P('layer', 'gy', 'gx'), may hold values from -1 to 1
- cell_init: float32 [2, 32, 2048, 256], P('layer', 'gy', 'gx'), may hold values from -5 to 5
- conv_weight: bfloat16 [2, 4608, 1024], P('layer'), may hold values from -0.09375 to 0.09375
- conv_bias: float32 [2, 1024], replicated, may hold values from -4 to 4
Outputs:
- hidden_out: bfloat16 [2, 32, 2048, 256], P('layer', 'gy', 'gx')
- cell_out: float32 [2, 32, 2048, 256], P('layer', 'gy', 'gx')
The draws below stay inside these ranges and needn't reach their ends.
All inputs are finite; a program needn't handle non-finite values.
Results may differ from the reference program's by a relative error of at most 0.0021.
Values may be sent and summed in bfloat16 or wider, within the bound.
No kernel may reach another device: no remote copies, remote signals or barrier semaphores. Data moves between devices by JAX's collectives and lax.ppermute only.
A program may use at most 128 MiB of HBM per device.

```python
import jax
import jax.numpy as jnp

C = 256
FRAMES = 2
LAYERS = 2
NY = 32
NX = 2048
GATES = 1024
KROWS = 4608


def block_scale(key, shape, shards, smallest, top_value):
    def one(position, shards_of):
        draws = jax.random.uniform(jax.random.fold_in(jax.random.fold_in(key, 6), position), (shards_of,), jnp.float32, smallest / len(shards), top_value / len(shards))
        return jnp.repeat(jnp.exp(draws), shape[position] // shards_of).reshape((-1,) + (1,) * (len(shape) - position - 1))

    level = one(*shards[0])
    for cut in shards[1:]:
        level = level * one(*cut)
    return level


def bell_draw(key, dims, deviation, bound, split=(), dtype=jnp.bfloat16):
    array = jax.random.normal(key, dims, jnp.float32) * deviation
    if len(split) > 0:
        array = block_scale(key, dims, split, -0.22, 0.18) * array
    return jnp.clip(array, min=-bound, max=bound).astype(dtype)


def setup_inputs(seed: int = 0) -> dict:
    keys = jax.random.split(jax.random.key(seed), 6)
    return {
        "frames": bell_draw(keys[0], (FRAMES, NY, NX, C), 1.0, 6.0, ((1, 8), (2, 8))),
        "hidden_init": jnp.clip(jax.random.uniform(keys[1], (LAYERS, NY, NX, C), jnp.float32, -1.0, 1.0) * block_scale(keys[1], (LAYERS, NY, NX, C), ((0, 2), (1, 8), (2, 8)), -0.4, 0.0), -1.0, 1.0).astype(jnp.bfloat16),
        "cell_init": bell_draw(keys[2], (LAYERS, NY, NX, C), 1.0, 5.0, ((0, 2), (1, 8), (2, 8)), jnp.float32),
        "conv_weight": bell_draw(keys[3], (LAYERS, KROWS, GATES), KROWS ** -0.5, 0.09375, ((0, 2),)),
        "conv_bias": bell_draw(keys[4], (LAYERS, GATES), 1.0, 4.0, (), jnp.float32),
    }


def gate_conv(joined, weight, bias):
    padded = jnp.pad(joined, ((1, 1), (1, 1), (0, 0)))
    rows_all, cols_all, width = joined.shape
    total = jnp.zeros((rows_all * cols_all, weight.shape[1]), jnp.float32)
    for tap in range(9):
        shift_y = tap // 3
        shift_x = tap % 3
        window = padded[shift_y:shift_y + rows_all, shift_x:shift_x + cols_all, :].reshape(-1, width)
        total = total + jnp.dot(window, weight[tap * width:(tap + 1) * width], preferred_element_type=jnp.float32)
    return total + bias[None, :]


def cell_update(gates, cell):
    chan = cell.shape[-1]
    gates = gates.reshape(cell.shape[0], cell.shape[1], 4 * chan)
    in_gate = jax.nn.sigmoid(gates[..., :chan])
    forget = jax.nn.sigmoid(gates[..., chan:2 * chan])
    out_gate = jax.nn.sigmoid(gates[..., 2 * chan:3 * chan])
    candidate = jnp.tanh(gates[..., 3 * chan:])
    new_cell = forget * cell + in_gate * candidate
    new_hidden = (out_gate * jnp.tanh(new_cell)).astype(jnp.bfloat16)
    return new_cell, new_hidden


def reference(frames, hidden_init, cell_init, conv_weight, conv_bias):
    hidden = [hidden_init[level] for level in range(LAYERS)]
    cell = [cell_init[level] for level in range(LAYERS)]
    for frame in range(FRAMES):
        source = frames[frame]
        for level in range(LAYERS):
            joined = jnp.concatenate([source, hidden[level]], axis=-1)
            gates = gate_conv(joined, conv_weight[level], conv_bias[level])
            cell[level], hidden[level] = cell_update(gates, cell[level])
            source = hidden[level]
    return jnp.stack(hidden), jnp.stack(cell)
```

```python
import jax
import jax.numpy as jnp
from jax import lax
from jax.experimental import pallas as pl
from jax.experimental.pallas import tpu as pltpu
from jax.sharding import PartitionSpec as P

f32 = jnp.float32
bf16 = jnp.bfloat16
ROWS, COLS, CH, GATES = 4, 256, 256, 1024
PAD = 8
EXT = COLS + 2 * PAD
LO, HI = 16, EXT - 16
NB = 512

ANYV = pl.BlockSpec(memory_space=pltpu.VMEM)
SM = pl.BlockSpec(memory_space=pltpu.SMEM)


def vm(shape, dtype):
    return pltpu.VMEM(shape, dtype)


def call(body, outs, args, aliases=None, scratch=(), flops=0, limit=14):
    specs = [SM] + [ANYV] * (len(args) - 1)
    return pl.pallas_call(
        body,
        in_specs=specs,
        out_specs=[ANYV] * len(outs),
        out_shape=list(outs),
        scratch_shapes=list(scratch),
        input_output_aliases=aliases or {},
        compiler_params=pltpu.CompilerParams(vmem_limit_bytes=limit << 20),
        cost_estimate=pl.CostEstimate(flops=flops, bytes_accessed=1 << 20, transcendentals=0),
    )(*args)


def shifted(x, store):
    n = x.shape[0]
    store(0, pltpu.roll(x, 1, 0).astype(bf16))
    store(1, x.astype(bf16))
    store(2, pltpu.roll(x, n - 1, 0).astype(bf16))


def build(stack, r, mid, left=None, right=None):
    mid = mid.astype(f32)
    if mid.shape[0] == COLS:
        zero = jnp.zeros((PAD, CH), f32)
        mid = jnp.concatenate([zero, mid, zero], axis=0)

    def store(dx, v):
        stack[dx, r] = v

    shifted(mid, store)


def columns(body):
    def step(n, carry):
        body(pl.ds(pl.multiple_of(n * NB, NB), NB))
        return carry

    lax.fori_loop(0, GATES // NB, step, 0)


def taps(w, c, lhs, off, tap, total):
    d = jnp.dot(lhs, w[pl.ds(tap * 512 + off, 256), c], preferred_element_type=f32)
    return d if total is None else total + d


def inner(acc, w, parts, c, lo, hi, add):
    for r in range(ROWS):
        total = acc[r, lo:hi, c] if add else None
        for dy in range(3):
            q = r + dy - 1
            if 0 <= q < ROWS:
                for dx in range(3):
                    for stack, off in parts:
                        total = taps(w, c, stack[dx, q, lo:hi, :], off, 3 * dy + dx, total)
        acc[r, lo:hi, c] = total


def outer(acc, w, parts, c, lo, hi):
    for r, q, dy in ((0, 0, 0), (ROWS - 1, 1, 2)):
        total = acc[r, lo:hi, c]
        for dx in range(3):
            for stack, off in parts:
                total = taps(w, c, stack[dx, q, lo:hi, :], off, 3 * dy + dx, total)
        acc[r, lo:hi, c] = total


def sigmoid(x):
    return 0.5 * jnp.tanh(0.5 * x) + 0.5


def epilogue(sc, acc, bias, cell_at, put):
    core, gx = sc[0], sc[1]
    b = bias[pl.ds(core, 1), :]

    def step(k, carry):
        at = pl.ds(pl.multiple_of(k * 16, 16), 16)
        col = lax.broadcasted_iota(jnp.int32, (16, CH), 0) + k * 16
        inside = jnp.logical_and(
            jnp.logical_or(gx > 0, col >= PAD), jnp.logical_or(gx < sc[2] - 1, col < PAD + COLS)
        )
        for r in range(ROWS):
            g = [acc[r, at, i * CH : (i + 1) * CH] + b[:, i * CH : (i + 1) * CH] for i in range(4)]
            cell = sigmoid(g[1]) * cell_at(r, at) + sigmoid(g[0]) * jnp.tanh(g[3])
            hid = sigmoid(g[2]) * jnp.tanh(cell)
            put(r, at, cell, jnp.where(inside, hid, 0.0))
        return carry

    lax.fori_loop(0, EXT // 16, step, 0)


def k_first(sc, fr, hid, w, acc_a, acc_b, s_f, s_h):
    core = sc[0]
    for r in range(ROWS):
        build(s_h, r, hid[0, r])

    @pl.when(core == 0)
    def _():
        for r in range(ROWS):
            build(s_f, r, fr[0, r])
        columns(lambda c: inner(acc_a, w, ((s_f, 0), (s_h, 256)), c, LO, HI, False))

    @pl.when(core == 1)
    def _():
        columns(lambda c: inner(acc_b, w, ((s_h, 256),), c, LO, HI, False))


def k_second(sc, fr, w, yt, yb, acc_a, acc_b, out_a, out_b, s_f, halo):
    core = sc[0]
    for i in range(3):
        build(halo.at[i], 0, yt[i])
        build(halo.at[i], 1, yb[i])

    @pl.when(core == 0)
    def _():
        for r in range(ROWS):
            build(s_f, r, fr[1, r])

        def body(c):
            outer(acc_a, w, ((halo.at[0], 0), (halo.at[2], 256)), c, LO, HI)
            inner(acc_b, w, ((s_f, 0),), c, LO, HI, False)
            outer(acc_b, w, ((halo.at[1], 0),), c, LO, HI)

        columns(body)

    @pl.when(core == 1)
    def _():
        columns(lambda c: outer(acc_b, w, ((halo.at[2], 256),), c, LO, HI))


def strip(s, i, rows, left, right):
    for r in range(ROWS + 2):
        row = rows(r)
        a = jnp.concatenate([left[i, r].astype(f32), row[0:16].astype(f32)], axis=0)
        b = jnp.concatenate([row[COLS - 16 : COLS].astype(f32), right[i, r].astype(f32)], axis=0)

        def store_a(dx, v):
            s[dx, r, 0:16, :] = v[0:16]

        def store_b(dx, v):
            s[dx, r, 16:32, :] = v[8:24]

        n = 24
        for dx, k in ((0, 1), (1, 0), (2, n - 1)):
            av = pltpu.roll(a, k, 0) if k else a
            bv = pltpu.roll(b, k, 0) if k else b
            s[dx, r, 0:16, :] = av[0:16].astype(bf16)
            s[dx, r, 16:32, :] = bv[8:24].astype(bf16)


def sides(acc, w, parts, c):
    total = None
    for dy in range(3):
        for dx in range(3):
            for s, off in parts:
                lhs = s[dx, dy : dy + ROWS].reshape(ROWS * 32, CH)
                total = taps(w, c, lhs, off, 3 * dy + dx, total)
    for r in range(ROWS):
        acc[r, 0:LO, c] = total[r * 32 : r * 32 + 16]
        acc[r, HI:EXT, c] = total[r * 32 + 16 : r * 32 + 32]


def k_sides(sc, fr, hid, cell, w, bias, yt, yb, left, right, cl, cr, acc_a, acc_b, out_a, out_b, h, cx, s):
    core = sc[0]

    def rows_of(i, tile):
        def rows(r):
            if r == 0:
                return yt[i]
            if r == ROWS + 1:
                return yb[i]
            return tile[r - 1]

        return rows

    strip(s.at[2], 2, rows_of(2, hid.at[0]), left, right)
    for r in range(ROWS):
        cx[r, 0:PAD] = cl[0, r].astype(f32) + cl[1, r].astype(f32)
        cx[r, PAD : PAD + COLS] = cell[0, r]
        cx[r, PAD + COLS : EXT] = cr[0, r].astype(f32) + cr[1, r].astype(f32)

    @pl.when(core == 0)
    def _():
        strip(s.at[0], 0, rows_of(0, fr.at[0]), left, right)
        strip(s.at[1], 1, rows_of(1, fr.at[1]), left, right)

        def body(c):
            sides(acc_a, w, ((s.at[0], 0), (s.at[2], 256)), c)
            sides(acc_b, w, ((s.at[1], 0),), c)

        columns(body)

        def put(r, at, new, hd):
            cx[r, at] = new
            h[r, at] = hd.astype(bf16)

        epilogue(sc, acc_a, bias, lambda r, at: cx[r, at], put)

    @pl.when(core == 1)
    def _():
        h[...] = jnp.zeros((ROWS, EXT, CH), bf16)
        columns(lambda c: sides(acc_b, w, ((s.at[2], 256),), c))


def k_third(sc, h, recv, w, acc_b, out_b, s):
    core = sc[0]

    @pl.when(core == 0)
    def _():
        for r in range(ROWS):
            build(s, r, h[r])

    @pl.when(core == 1)
    def _():
        for r in range(ROWS):
            build(s, r, recv[r])

    off = pl.multiple_of((1 - core) * 256, 256)
    columns(lambda c: inner(acc_b, w, ((s, off),), c, 0, EXT, True))


def k_fourth(sc, top, bot, w, bias, cx, acc_b, out_b, h, cx2, s):
    core = sc[0]
    build(s, 0, top[...])
    build(s, 1, bot[...])
    off = pl.multiple_of((1 - core) * 256, 256)
    columns(lambda c: outer(acc_b, w, ((s, off),), c, 0, EXT))

    def put(r, at, new, hd):
        cx2[r, at] = new
        h[r, at] = hd.astype(bf16)

    epilogue(sc, acc_b, bias, lambda r, at: cx[r, at], put)


def k_fifth(sc, h, w, acc, s):
    @pl.when(sc[0] == 1)
    def _():
        for r in range(ROWS):
            build(s, r, h[r])
        columns(lambda c: inner(acc, w, ((s, 256),), c, 0, EXT, False))


def k_sixth(sc, top, bot, w, acc, out, s):
    @pl.when(sc[0] == 1)
    def _():
        build(s, 0, top[...])
        build(s, 1, bot[...])
        columns(lambda c: outer(acc, w, ((s, 256),), c, 0, EXT))


def k_last(sc, recv, h, cx, w, bias, acc, out, ho, co, s, s2):
    core = sc[0]

    @pl.when(core == 0)
    def _():
        for r in range(ROWS):
            ho[0, r] = h[r].astype(f32)[PAD : PAD + COLS].astype(bf16)
            co[0, r] = cx[r, PAD : PAD + COLS]

    @pl.when(core == 1)
    def _():
        for r in range(ROWS):
            build(s, r, recv[r + 1])
        build(s2, 0, recv[0])
        build(s2, 1, recv[ROWS + 1])

        def body(c):
            inner(acc, w, ((s, 0),), c, 0, EXT, True)
            outer(acc, w, ((s2, 0),), c, 0, EXT)

        columns(body)
        b = bias[pl.ds(core, 1), :]

        def step(k, carry):
            at = pl.ds(pl.multiple_of(k * 16, 16), 16)
            src = pl.ds(pl.multiple_of(k * 16 + PAD, 8), 16)
            for r in range(ROWS):
                g = [acc[r, src, i * CH : (i + 1) * CH] + b[:, i * CH : (i + 1) * CH] for i in range(4)]
                new = sigmoid(g[1]) * cx[r, src] + sigmoid(g[0]) * jnp.tanh(g[3])
                co[0, r, at] = new
                ho[0, r, at] = (sigmoid(g[2]) * jnp.tanh(new)).astype(bf16)
            return carry

        lax.fori_loop(0, COLS // 16, step, 0)


UNIT = 2 * ROWS * COLS * 4608 * 1024
ACC = (ROWS, EXT, GATES)
TILE = (ROWS, EXT, CH)
STACK = (3, ROWS, EXT, CH)
PAIR = (3, 2, EXT, CH)


def along(axis, count):
    up = [(i, i + 1) for i in range(count - 1)]
    return up, [(b, a) for a, b in up]


def per_device(frames, hidden_init, cell_init, conv_weight, conv_bias):
    core = lax.axis_index("layer")
    ny, nx = lax.axis_size("gy"), lax.axis_size("gx")
    sc = jnp.stack([core, lax.axis_index("gx"), jnp.int32(nx)]).astype(jnp.int32)
    w = pltpu.with_memory_space_constraint(conv_weight[0], pltpu.VMEM)
    down, up = along("gy", ny)
    right, left = along("gx", nx)
    swap = [(0, 1), (1, 0)]

    def edge_rows(r):
        return jnp.concatenate([frames[:, r], hidden_init[:, r]], axis=0)

    yt = lax.ppermute(edge_rows(ROWS - 1), "gy", down)
    yb = lax.ppermute(edge_rows(0), "gy", up)

    acc_a, acc_b = call(
        k_first,
        [vm(ACC, f32), vm(ACC, f32)],
        [sc, frames, hidden_init, w],
        scratch=[pltpu.VMEM(STACK, bf16)] * 2,
        flops=int(UNIT * 0.75),
    )

    hi = lax.reduce_precision(cell_init[0], 8, 7)
    rest = cell_init[0] - hi

    def edge_cols(a, b):
        six = jnp.concatenate(
            [
                yt[:, None, a:b],
                jnp.concatenate([frames[:, :, a:b], hidden_init[:, :, a:b]], axis=0),
                yb[:, None, a:b],
            ],
            axis=1,
        ).reshape(18, b - a, CH)
        return jnp.concatenate([six, hi[:, a:b].astype(bf16), rest[:, a:b].astype(bf16)], axis=0)

    from_left = lax.ppermute(edge_cols(COLS - PAD, COLS), "gx", right)
    from_right = lax.ppermute(edge_cols(0, PAD), "gx", left)

    acc_a, acc_b = call(
        k_second,
        [vm(ACC, f32), vm(ACC, f32)],
        [sc, frames, w, yt, yb, acc_a, acc_b],
        aliases={5: 0, 6: 1},
        scratch=[pltpu.VMEM(STACK, bf16), pltpu.VMEM((3,) + PAIR, bf16)],
        flops=int(UNIT * 0.55),
    )

    def six_of(m):
        return m[:18].reshape(3, 6, PAD, CH), m[18:].reshape(2, ROWS, PAD, CH)

    l6, cl = six_of(from_left)
    r6, cr = six_of(from_right)
    acc_a, acc_b, h, cx = call(
        k_sides,
        [vm(ACC, f32), vm(ACC, f32), vm(TILE, bf16), vm(TILE, f32)],
        [sc, frames, hidden_init, cell_init, w, conv_bias, yt, yb, l6, r6, cl, cr, acc_a, acc_b],
        aliases={12: 0, 13: 1},
        scratch=[pltpu.VMEM((3, 3, 6, 32, CH), bf16)],
        flops=int(UNIT * 0.25),
        limit=20,
    )

    recv = lax.ppermute(h, "layer", swap)
    src = jnp.where(core == 0, h, recv)
    top = lax.ppermute(src[ROWS - 1], "gy", down)
    bot = lax.ppermute(src[0], "gy", up)
    (acc_b,) = call(
        k_third,
        [vm(ACC, f32)],
        [sc, h, recv, w, acc_b],
        aliases={4: 0},
        scratch=[pltpu.VMEM(STACK, bf16)],
        flops=int(UNIT * 0.42),
    )
    acc_b, h2, cx2 = call(
        k_fourth,
        [vm(ACC, f32), vm(TILE, bf16), vm(TILE, f32)],
        [sc, top, bot, w, conv_bias, cx, acc_b],
        aliases={6: 0},
        scratch=[pltpu.VMEM(PAIR, bf16)],
        flops=int(UNIT * 0.16),
    )

    top2 = lax.ppermute(h2[ROWS - 1], "gy", down)
    bot2 = lax.ppermute(h2[0], "gy", up)
    (acc,) = call(
        k_fifth,
        [vm(ACC, f32)],
        [sc, h2, w],
        scratch=[pltpu.VMEM(STACK, bf16)],
        flops=int(UNIT * 0.42),
    )
    (acc,) = call(
        k_sixth,
        [vm(ACC, f32)],
        [sc, top2, bot2, w, acc],
        aliases={4: 0},
        scratch=[pltpu.VMEM(PAIR, bf16)],
        flops=int(UNIT * 0.08),
    )
    six = jnp.concatenate([top2[None], h2, bot2[None]], axis=0)
    six, acc = lax.optimization_barrier((six, acc))
    recv2 = lax.ppermute(six, "layer", swap)
    acc, ho, co = call(
        k_last,
        [
            vm(ACC, f32),
            jax.ShapeDtypeStruct((1, ROWS, COLS, CH), bf16),
            jax.ShapeDtypeStruct((1, ROWS, COLS, CH), f32),
        ],
        [sc, recv2, h2, cx2, w, conv_bias, acc],
        aliases={6: 0},
        scratch=[pltpu.VMEM(STACK, bf16), pltpu.VMEM(PAIR, bf16)],
        flops=int(UNIT * 0.5),
    )
    return ho, co


def solution(mesh):
    placed = (
        P(None, "gy", "gx", None),
        P("layer", "gy", "gx", None),
        P("layer", "gy", "gx", None),
        P("layer", None, None),
        P(),
    )
    return jax.shard_map(
        per_device,
        mesh=mesh,
        in_specs=placed,
        out_specs=(P("layer", "gy", "gx", None), P("layer", "gy", "gx", None)),
        check_vma=False,
    )
```

```python
import jax
import jax.numpy as jnp
from jax import lax
from jax.experimental import pallas as pl
from jax.experimental.pallas import tpu as pltpu
from jax.sharding import PartitionSpec as P

f32 = jnp.float32
bf16 = jnp.bfloat16
ROWS, COLS, CH, GATES = 4, 256, 256, 1024
PAD = 8
EXT = COLS + 2 * PAD
LO, HI = 16, EXT - 16
NB = 512
UNIT = 2 * ROWS * COLS * 4608 * 1024
ACC = (ROWS, EXT, GATES)
TILE = (ROWS, EXT, CH)
STACK = (3, ROWS, EXT, CH)
PAIR = (3, 2, EXT, CH)
EDGE = (20, PAD, CH)

ANYV = pl.BlockSpec(memory_space=pltpu.VMEM)


def vm(shape, dtype):
    return pltpu.VMEM(shape, dtype)


def call(body, outs, args, aliases=None, scratch=(), part=0.0, limit=8):
    return pl.pallas_call(
        body,
        in_specs=[ANYV] * len(args),
        out_specs=[ANYV] * len(outs),
        out_shape=list(outs),
        scratch_shapes=list(scratch),
        input_output_aliases=aliases or {},
        compiler_params=pltpu.CompilerParams(vmem_limit_bytes=limit << 20),
        cost_estimate=pl.CostEstimate(flops=int(UNIT * part), bytes_accessed=1 << 20, transcendentals=0),
    )(*args)


def core_is(k):
    return pl.when(lax.axis_index("layer") == k)


def inside(axis, step):
    at = lax.axis_index(axis) + step
    return jnp.logical_and(at >= 0, at < lax.axis_size(axis)).astype(f32)


def build(stack, r, x):
    x = x.astype(f32)
    stack[0, r] = pltpu.roll(x, 1, 0).astype(bf16)
    stack[1, r] = x.astype(bf16)
    stack[2, r] = pltpu.roll(x, EXT - 1, 0).astype(bf16)


def widen(row, left, right):
    a = left.astype(f32) * inside("gx", -1)
    b = right.astype(f32) * inside("gx", 1)
    return jnp.concatenate([a, row.astype(f32), b], axis=0)


def bare(row):
    zero = jnp.zeros((PAD, CH), f32)
    return jnp.concatenate([zero, row.astype(f32), zero], axis=0)


def columns(body):
    def step(n, carry):
        body(pl.ds(pl.multiple_of(n * NB, NB), NB))
        return carry

    lax.fori_loop(0, GATES // NB, step, 0)


def taps(w, c, lhs, off, tap, total):
    d = jnp.dot(lhs, w[pl.ds(tap * 512 + off, 256), c], preferred_element_type=f32)
    return d if total is None else total + d


def inner(acc, w, stack, off, c, lo, hi, add):
    for r in range(ROWS):
        total = acc[r, lo:hi, c] if add else None
        for dy in range(3):
            q = r + dy - 1
            if 0 <= q < ROWS:
                for dx in range(3):
                    total = taps(w, c, stack[dx, q, lo:hi, :], off, 3 * dy + dx, total)
        acc[r, lo:hi, c] = total


def outer(acc, w, parts, c):
    for r, q, dy in ((0, 0, 0), (ROWS - 1, 1, 2)):
        total = acc[r, :, c]
        for dx in range(3):
            for stack, off in parts:
                total = taps(w, c, stack[dx, q], off, 3 * dy + dx, total)
        acc[r, :, c] = total


def sigmoid(x):
    return 0.5 * jnp.tanh(0.5 * x) + 0.5


def gates_at(acc, b, r, at, cell):
    g = [acc[r, at, i * CH : (i + 1) * CH] + b[:, i * CH : (i + 1) * CH] for i in range(4)]
    cell = sigmoid(g[1]) * cell + sigmoid(g[0]) * jnp.tanh(g[3])
    return cell, sigmoid(g[2]) * jnp.tanh(cell)


def epilogue(acc, bias, layer, cell_in, cell_out, h):
    b = bias[layer : layer + 1, :]
    first = PAD * (1 - inside("gx", -1)).astype(jnp.int32)
    last = EXT - PAD * (1 - inside("gx", 1)).astype(jnp.int32)

    def step(k, carry):
        at = pl.ds(pl.multiple_of(k * 16, 16), 16)
        col = lax.broadcasted_iota(jnp.int32, (16, CH), 0) + k * 16
        keep = jnp.logical_and(col >= first, col < last)
        for r in range(ROWS):
            new, hid = gates_at(acc, b, r, at, cell_in[r, at])
            cell_out[r, at] = new
            h[r, at] = jnp.where(keep, hid, 0.0).astype(bf16)
        return carry

    lax.fori_loop(0, EXT // 16, step, 0)


def k_edges(fr, hid, cell, to_left, to_right):
    for out, a in ((to_left, 0), (to_right, COLS - PAD)):
        for r in range(ROWS):
            out[r] = fr[0, r, a : a + PAD]
            out[4 + r] = fr[1, r, a : a + PAD]
            out[8 + r] = hid[0, r, a : a + PAD]
            c = cell[0, r, a : a + PAD]
            hi = c.astype(bf16)
            out[12 + r] = hi
            out[16 + r] = (c - hi.astype(f32)).astype(bf16)


def k_hidden(hid, w, acc, s):
    for r in range(ROWS):
        build(s, r, bare(hid[0, r]))
    columns(lambda c: inner(acc, w, s, 256, c, LO, HI, False))


def k_rows(fr, hid, left, right, up, down):
    for out, r in ((up, 0), (down, ROWS - 1)):
        for i in range(3):
            row = hid[0, r] if i == 2 else fr[i, r]
            out[i] = widen(row, left[4 * i + r], right[4 * i + r]).astype(bf16)


def k_frames(fr, hid, cell, w, left, right, acc_in, acc, acc_b, cx, s, t):
    for r in range(ROWS):
        a = left[12 + r].astype(f32) + left[16 + r].astype(f32)
        b = right[12 + r].astype(f32) + right[16 + r].astype(f32)
        cx[r] = jnp.concatenate([a, cell[0, r], b], axis=0)
        x = widen(hid[0, r], left[8 + r], right[8 + r])
        for dx, y in ((0, pltpu.roll(x, 1, 0)), (1, x), (2, pltpu.roll(x, EXT - 1, 0))):
            t[dx, r, 0:16] = y[0:16].astype(bf16)
            t[dx, r, 16:32] = y[HI:EXT].astype(bf16)

    def sides(c):
        total = None
        for dy in range(3):
            n = ROWS if dy == 1 else ROWS - 1
            first = max(dy - 1, 0)
            for dx in range(3):
                lhs = t[dx, first : first + n].reshape(n * 32, CH)
                d = jnp.dot(lhs, w[pl.ds((3 * dy + dx) * 512 + 256, 256), c], preferred_element_type=f32)
                zero = jnp.zeros((32, NB), f32)
                if dy == 0:
                    d = jnp.concatenate([zero, d], axis=0)
                if dy == 2:
                    d = jnp.concatenate([d, zero], axis=0)
                total = d if total is None else total + d
        for r in range(ROWS):
            acc[r, 0:LO, c] = total[r * 32 : r * 32 + 16]
            acc[r, HI:EXT, c] = total[r * 32 + 16 : r * 32 + 32]

    columns(sides)

    @core_is(0)
    def _():
        for r in range(ROWS):
            build(s, r, widen(fr[0, r], left[r], right[r]))
        columns(lambda c: inner(acc, w, s, 0, c, 0, EXT, True))
        for r in range(ROWS):
            build(s, r, widen(fr[1, r], left[4 + r], right[4 + r]))
        columns(lambda c: inner(acc_b, w, s, 0, c, 0, EXT, False))


def halo(s, top, bot):
    build(s, 0, top.astype(f32) * inside("gy", -1))
    build(s, 1, bot.astype(f32) * inside("gy", 1))


def k_first(top, bot, w, bias, cx_in, acc_in, acc, h, cx, s):
    halo(s.at[1], top[2], bot[2])

    @core_is(0)
    def _():
        halo(s.at[0], top[0], bot[0])
        columns(lambda c: outer(acc, w, ((s.at[0], 0), (s.at[1], 256)), c))
        epilogue(acc, bias, 0, cx, cx, h)

    @core_is(1)
    def _():
        columns(lambda c: outer(acc, w, ((s.at[1], 256),), c))


def k_second(top, bot, w, acc_in, acc, s):
    @core_is(0)
    def _():
        halo(s, top[1], bot[1])
        columns(lambda c: outer(acc, w, ((s, 0),), c))


def k_pick(h, recv, up, down):
    @core_is(0)
    def _():
        up[...] = h[0]
        down[...] = h[ROWS - 1]

    @core_is(1)
    def _():
        up[...] = recv[0]
        down[...] = recv[ROWS - 1]


def k_third(h, recv, w, a_in, b_in, acc_a, acc_b, s):
    @core_is(0)
    def _():
        for r in range(ROWS):
            build(s, r, h[r])
        columns(lambda c: inner(acc_b, w, s, 256, c, 0, EXT, True))

    @core_is(1)
    def _():
        for r in range(ROWS):
            build(s, r, recv[r])
        columns(lambda c: inner(acc_a, w, s, 0, c, 0, EXT, True))


def k_fourth(top, bot, w, bias, cx_in, a_in, b_in, acc_a, acc_b, cx, h, up, down, s):
    halo(s, top[...], bot[...])

    @core_is(0)
    def _():
        columns(lambda c: outer(acc_b, w, ((s, 256),), c))
        epilogue(acc_b, bias, 0, cx, cx, h)

    @core_is(1)
    def _():
        columns(lambda c: outer(acc_a, w, ((s, 0),), c))
        epilogue(acc_a, bias, 1, cx, cx, h)

    up[...] = h[0]
    down[...] = h[ROWS - 1]


def k_fifth(h, w, acc_in, acc, s):
    @core_is(1)
    def _():
        for r in range(ROWS):
            build(s, r, h[r])
        columns(lambda c: inner(acc, w, s, 256, c, 0, EXT, False))


def k_sixth(top, bot, w, acc_in, acc, out, s):
    @core_is(0)
    def _():
        out[0] = top[...]
        out[1] = bot[...]

    @core_is(1)
    def _():
        halo(s, top[...], bot[...])
        columns(lambda c: outer(acc, w, ((s, 256),), c))


def k_seventh(recv, w, acc_in, acc, s):
    @core_is(1)
    def _():
        for r in range(ROWS):
            build(s, r, recv[r])
        columns(lambda c: inner(acc, w, s, 0, c, 0, EXT, True))


def k_last(two, h, cx, w, bias, acc_in, acc, ho, co, s):
    @core_is(0)
    def _():
        for r in range(ROWS):
            ho[0, r] = h[r].astype(f32)[PAD : PAD + COLS].astype(bf16)
            co[0, r] = cx[r, PAD : PAD + COLS]

    @core_is(1)
    def _():
        halo(s, two[0], two[1])
        columns(lambda c: outer(acc, w, ((s, 0),), c))
        b = bias[1:2, :]

        def step(k, carry):
            at = pl.ds(pl.multiple_of(k * 16, 16), 16)
            src = pl.ds(pl.multiple_of(k * 16 + PAD, 8), 16)
            for r in range(ROWS):
                new, hid = gates_at(acc, b, r, src, cx[r, src])
                co[0, r, at] = new
                ho[0, r, at] = hid.astype(bf16)
            return carry

        lax.fori_loop(0, COLS // 16, step, 0)


def both_ways(axis, to_low, to_high):
    n = lax.axis_size(axis)
    from_low = lax.ppermute(to_high, axis, [(i, (i + 1) % n) for i in range(n)])
    from_high = lax.ppermute(to_low, axis, [(i, (i - 1) % n) for i in range(n)])
    return from_low, from_high


def per_device(frames, hidden_init, cell_init, conv_weight, conv_bias):
    w = pltpu.with_memory_space_constraint(conv_weight[0], pltpu.VMEM)
    bias = conv_bias
    swap = [(0, 1), (1, 0)]

    edge = vm(EDGE, bf16)
    to_left, to_right = call(k_edges, [edge, edge], [frames, hidden_init, cell_init])
    left, right = both_ways("gx", to_left, to_right)
    (acc_a,) = call(k_hidden, [vm(ACC, f32)], [hidden_init, w], scratch=[pltpu.VMEM(STACK, bf16)], part=0.4)

    rows = vm((3, EXT, CH), bf16)
    to_up, to_down = call(k_rows, [rows, rows], [frames, hidden_init, left, right])
    top, bot = both_ways("gy", to_up, to_down)
    acc_a, acc_b, cx = call(
        k_frames,
        [vm(ACC, f32), vm(ACC, f32), vm(TILE, f32)],
        [frames, hidden_init, cell_init, w, left, right, acc_a],
        aliases={6: 0},
        scratch=[pltpu.VMEM(STACK, bf16), pltpu.VMEM((3, ROWS, 32, CH), bf16)],
        part=0.95,
    )
    acc_a, h, cx = call(
        k_first,
        [vm(ACC, f32), vm(TILE, bf16), vm(TILE, f32)],
        [top, bot, w, bias, cx, acc_a],
        aliases={5: 0, 4: 2},
        scratch=[pltpu.VMEM((2,) + PAIR, bf16)],
        part=0.3,
    )

    recv = lax.ppermute(h, "layer", swap)
    (acc_b,) = call(
        k_second, [vm(ACC, f32)], [top, bot, w, acc_b], aliases={3: 0}, scratch=[pltpu.VMEM(PAIR, bf16)], part=0.1
    )
    row = vm((EXT, CH), bf16)
    to_up, to_down = call(k_pick, [row, row], [h, recv])
    top, bot = both_ways("gy", to_up, to_down)
    acc_a, acc_b = call(
        k_third,
        [vm(ACC, f32), vm(ACC, f32)],
        [h, recv, w, acc_a, acc_b],
        aliases={3: 0, 4: 1},
        scratch=[pltpu.VMEM(STACK, bf16)],
        part=0.45,
    )
    acc_a, acc_b, cx, h, to_up, to_down = call(
        k_fourth,
        [vm(ACC, f32), vm(ACC, f32), vm(TILE, f32), vm(TILE, bf16), row, row],
        [top, bot, w, bias, cx, acc_a, acc_b],
        aliases={4: 2, 5: 0, 6: 1},
        scratch=[pltpu.VMEM(PAIR, bf16)],
        part=0.3,
    )

    top, bot = both_ways("gy", to_up, to_down)
    recv = lax.ppermute(h, "layer", swap)
    (acc_b,) = call(
        k_fifth, [vm(ACC, f32)], [h, w, acc_b], aliases={2: 0}, scratch=[pltpu.VMEM(STACK, bf16)], part=0.45
    )
    acc_b, two = call(
        k_sixth,
        [vm(ACC, f32), vm((2, EXT, CH), bf16)],
        [top, bot, w, acc_b],
        aliases={3: 0},
        scratch=[pltpu.VMEM(PAIR, bf16)],
        part=0.1,
    )
    two = lax.ppermute(two, "layer", swap)
    (acc_b,) = call(
        k_seventh, [vm(ACC, f32)], [recv, w, acc_b], aliases={2: 0}, scratch=[pltpu.VMEM(STACK, bf16)], part=0.45
    )
    _, ho, co = call(
        k_last,
        [
            vm(ACC, f32),
            jax.ShapeDtypeStruct((1, ROWS, COLS, CH), bf16),
            jax.ShapeDtypeStruct((1, ROWS, COLS, CH), f32),
        ],
        [two, h, cx, w, bias, acc_b],
        aliases={5: 0},
        scratch=[pltpu.VMEM(PAIR, bf16)],
        part=0.3,
    )
    return ho, co


def solution(mesh):
    placed = (
        P(None, "gy", "gx", None),
        P("layer", "gy", "gx", None),
        P("layer", "gy", "gx", None),
        P("layer", None, None),
        P(),
    )
    return jax.shard_map(
        per_device,
        mesh=mesh,
        in_specs=placed,
        out_specs=(P("layer", "gy", "gx", None), P("layer", "gy", "gx", None)),
        check_vma=False,
    )
```

```python
import jax
import jax.numpy as jnp
from jax import lax
from jax.experimental import pallas as pl
from jax.experimental.pallas import tpu as pltpu
from jax.sharding import PartitionSpec as P

f32 = jnp.float32
bf16 = jnp.bfloat16
ROWS, COLS, CH, GATES = 4, 256, 256, 1024
PAD = 8
EXT = COLS + 2 * PAD
LO, HI = 16, EXT - 16
NB = 512
UNIT = 2 * ROWS * COLS * 4608 * 1024
ACC = (ROWS, EXT, GATES)
TILE = (ROWS, EXT, CH)
STACK = (3, ROWS, EXT, CH)
PAIR = (3, 2, EXT, CH)
EDGE = (20, PAD, CH)

CENTER = (3, ROWS, COLS, CH)
GROUP = CH // 2

ANYV = pl.BlockSpec(memory_space=pltpu.VMEM)
HBM = pl.BlockSpec(memory_space=pltpu.HBM)


def vm(shape, dtype):
    return pltpu.VMEM(shape, dtype)


def call(body, outs, args, aliases=None, scratch=(), part=0.0, limit=8, far=(), far_out=()):
    return pl.pallas_call(
        body,
        in_specs=[HBM if i in far else ANYV for i in range(len(args))],
        out_specs=[HBM if i in far_out else ANYV for i in range(len(outs))],
        out_shape=list(outs),
        scratch_shapes=list(scratch),
        input_output_aliases=aliases or {},
        compiler_params=pltpu.CompilerParams(vmem_limit_bytes=limit << 20),
        cost_estimate=pl.CostEstimate(flops=int(UNIT * part), bytes_accessed=1 << 20, transcendentals=0),
    )(*args)


def far(x):
    return pltpu.with_memory_space_constraint(x, pltpu.HBM)


def core_is(k):
    return pl.when(lax.axis_index("layer") == k)


def inside(axis, step):
    at = lax.axis_index(axis) + step
    return jnp.logical_and(at >= 0, at < lax.axis_size(axis)).astype(f32)


def build(stack, r, x):
    x = x.astype(f32)
    stack[0, r] = pltpu.roll(x, 1, 0).astype(bf16)
    stack[1, r] = x.astype(bf16)
    stack[2, r] = pltpu.roll(x, EXT - 1, 0).astype(bf16)


def widen(row, left, right):
    a = left.astype(f32) * inside("gx", -1)
    b = right.astype(f32) * inside("gx", 1)
    return jnp.concatenate([a, row.astype(f32), b], axis=0)


def bare(row):
    zero = jnp.zeros((PAD, CH), f32)
    return jnp.concatenate([zero, row.astype(f32), zero], axis=0)


def build_center(stack, r, x):
    x = x.astype(f32)
    for dx, y in ((0, pltpu.roll(x, 1, 0)), (1, x), (2, pltpu.roll(x, EXT - 1, 0))):
        stack[dx, r] = y[PAD : PAD + COLS].astype(bf16)


BLOCKS = range(GATES // NB)


def taps(w, n, lhs, off, tap, total):
    d = jnp.dot(lhs, w[tap, off : off + 256, n * NB : (n + 1) * NB], preferred_element_type=f32)
    return d if total is None else total + d


def inner(acc, w, stack, off, n, r, lo, hi, add):
    c = slice(n * NB, (n + 1) * NB)
    total = acc[r, lo:hi, c] if add else None
    for dy in range(3):
        q = r + dy - 1
        if 0 <= q < ROWS:
            for dx in range(3):
                total = taps(w, n, stack[dx, q, lo:hi, :], off, 3 * dy + dx, total)
    acc[r, lo:hi, c] = total


ENDS = ((0, 0, 0), (ROWS - 1, 1, 2))


def outer(acc, w, parts, n, end, m=EXT):
    r, q, dy = ENDS[end]
    c = slice(n * NB, (n + 1) * NB)
    total = acc[r, 0:m, c]
    for dx in range(3):
        for stack, off in parts:
            total = taps(w, n, stack[dx, q], off, 3 * dy + dx, total)
    acc[r, 0:m, c] = total


def sigmoid(x):
    return 0.5 * jnp.tanh(0.5 * x) + 0.5


def gates_at(acc, bias, layer, r, n, at, cell):
    def gate(i):
        b = bias[layer : layer + 1, i * CH + n * GROUP : i * CH + (n + 1) * GROUP]
        return acc[r, at, n * NB + i * GROUP : n * NB + (i + 1) * GROUP] + b

    cell = sigmoid(gate(1)) * cell + sigmoid(gate(0)) * jnp.tanh(gate(3))
    return cell, sigmoid(gate(2)) * jnp.tanh(cell)


def finish(acc, bias, layer, r, n, cx, h):
    ch = slice(n * GROUP, (n + 1) * GROUP)
    for k in range(EXT // 16):
        at = slice(k * 16, (k + 1) * 16)
        new, hid = gates_at(acc, bias, layer, r, n, at, cx[r, at, ch])
        cx[r, at, ch] = new
        if k in (0, EXT // 16 - 1):
            half = lax.broadcasted_iota(jnp.int32, (16, GROUP), 0) < PAD
            kept = half if k else jnp.logical_not(half)
            hid = hid * jnp.where(kept, 1.0, inside("gx", 1 if k else -1))
        h[r, at, ch] = hid.astype(bf16)


def finish_center(acc, bias, r, n, cx, hv, cv):
    ch = slice(n * GROUP, (n + 1) * GROUP)
    for k in range(COLS // 16):
        at = slice(k * 16, (k + 1) * 16)
        src = slice(k * 16 + PAD, (k + 1) * 16 + PAD)
        new, hid = gates_at(acc, bias, 1, r, n, at, cx[r, src, ch])
        cv[r, at, ch] = new
        hv[r, at, ch] = hid.astype(bf16)


def k_edges(fr, hid, cell, to_left, to_right, fs, hs, cs, sem):
    jobs = []
    for side, a in ((0, 0), (1, COLS - 16)):
        jobs.append((fr.at[:, :, a : a + 16, :], fs.at[side]))
        jobs.append((hid.at[0, :, a : a + 16, :], hs.at[side]))
        jobs.append((cell.at[0, :, a : a + 16, :], cs.at[side]))
    copies = [pltpu.make_async_copy(src, dst, sem.at[i]) for i, (src, dst) in enumerate(jobs)]
    for c in copies:
        c.start()
    for c in copies:
        c.wait()
    for side, out, at in ((0, to_left, slice(0, PAD)), (1, to_right, slice(PAD, 16))):
        for r in range(ROWS):
            out[r] = fs[side, 0, r, at]
            out[4 + r] = fs[side, 1, r, at]
            out[8 + r] = hs[side, r, at]
            c = cs[side, r, at]
            hi = c.astype(bf16)
            out[12 + r] = hi
            out[16 + r] = (c - hi.astype(f32)).astype(bf16)


def k_hidden(hid, w_far, w, acc, s, hv, sem):
    copies = {}
    for part in (1, 0):
        for n in BLOCKS:
            for i in range(4):
                rows = slice(part * 256, part * 256 + 256)
                src = w_far.at[:, rows, i * CH + n * GROUP : i * CH + (n + 1) * GROUP]
                dst = w.at[:, rows, n * NB + i * GROUP : n * NB + (i + 1) * GROUP]
                copies[part, n, i] = pltpu.make_async_copy(src, dst, sem.at[part, n, i])
    own = pltpu.make_async_copy(hid.at[0], hv, sem.at[2, 0, 0])
    own.start()
    for c in copies.values():
        c.start()
    own.wait()
    for r in range(ROWS):
        build(s, r, bare(hv[r]))
    for n in BLOCKS:
        for i in range(4):
            copies[1, n, i].wait()
        for r in range(ROWS):
            inner(acc, w, s, 256, n, r, LO, HI, False)
    for n in BLOCKS:
        for i in range(4):
            copies[0, n, i].wait()


def k_rows(fr, hid, left, right, up, down):
    for out, r in ((up, 0), (down, ROWS - 1)):
        for i in range(3):
            row = hid[0, r] if i == 2 else fr[i, r]
            out[i] = widen(row, left[4 * i + r], right[4 * i + r]).astype(bf16)


def k_frames(fr, hid, cell, w, bias, left, right, acc_in, acc, acc_b, cx, h, s, t):
    for r in range(ROWS):
        a = left[12 + r].astype(f32) + left[16 + r].astype(f32)
        b = right[12 + r].astype(f32) + right[16 + r].astype(f32)
        cx[r] = jnp.concatenate([a, cell[0, r], b], axis=0)
        x = widen(hid[0, r], left[8 + r], right[8 + r])
        for dx, y in ((0, pltpu.roll(x, 1, 0)), (1, x), (2, pltpu.roll(x, EXT - 1, 0))):
            t[dx, r, 0:16] = y[0:16].astype(bf16)
            t[dx, r, 16:32] = y[HI:EXT].astype(bf16)

    def sides(n):
        c = slice(n * NB, (n + 1) * NB)
        total = None
        for dy in range(3):
            m = ROWS if dy == 1 else ROWS - 1
            first = max(dy - 1, 0)
            for dx in range(3):
                lhs = t[dx, first : first + m].reshape(m * 32, CH)
                d = taps(w, n, lhs, 256, 3 * dy + dx, None)
                zero = jnp.zeros((32, NB), f32)
                if dy == 0:
                    d = jnp.concatenate([zero, d], axis=0)
                if dy == 2:
                    d = jnp.concatenate([d, zero], axis=0)
                total = d if total is None else total + d
        for r in range(ROWS):
            acc[r, 0:LO, c] = total[r * 32 : r * 32 + 16]
            acc[r, HI:EXT, c] = total[r * 32 + 16 : r * 32 + 32]

    @core_is(1)
    def _():
        h[...] = jnp.zeros(TILE, bf16)
        for n in BLOCKS:
            sides(n)

    @core_is(0)
    def _():
        def frame(i, r):
            build(s.at[i], r, widen(fr[i, r], left[4 * i + r], right[4 * i + r]))

        for r in range(ROWS):
            frame(0, r)
        for n in BLOCKS:
            sides(n)
        for n in BLOCKS:
            for r in range(ROWS):
                inner(acc, w, s.at[0], 0, n, r, 0, EXT, True)
                if n == 0:
                    frame(1, r)
        for n in BLOCKS:
            for r in range(ROWS):
                inner(acc_b, w, s.at[1], 0, n, r, 0, EXT, False)
                if r in (1, 2):
                    finish(acc, bias, 0, r, n, cx, h)


def halo(s, top, bot):
    build(s, 0, top.astype(f32) * inside("gy", -1))
    build(s, 1, bot.astype(f32) * inside("gy", 1))


def k_first(top, bot, w, bias, cx_in, h_in, acc_in, acc, h, cx, s):
    halo(s.at[1], top[2], bot[2])

    @core_is(0)
    def _():
        halo(s.at[0], top[0], bot[0])
        for end in (0, 1):
            for n in BLOCKS:
                outer(acc, w, ((s.at[0], 0), (s.at[1], 256)), n, end)
        for end in (0, 1):
            for n in BLOCKS:
                finish(acc, bias, 0, ENDS[end][0], n, cx, h)

    @core_is(1)
    def _():
        for end in (0, 1):
            for n in BLOCKS:
                outer(acc, w, ((s.at[1], 256),), n, end)


def k_second(top, bot, w, acc_in, acc, s):
    @core_is(0)
    def _():
        halo(s, top[1], bot[1])
        for end in (0, 1):
            for n in BLOCKS:
                outer(acc, w, ((s, 0),), n, end)


def k_pick(h, recv, up, down):
    @core_is(0)
    def _():
        up[...] = h[0]
        down[...] = h[ROWS - 1]

    @core_is(1)
    def _():
        up[...] = recv[0]
        down[...] = recv[ROWS - 1]


def k_third(h_in, recv, w, bias, cx_in, a_in, b_in, acc_a, acc_b, cx, h, s):
    def work(src, acc, off, layer):
        build(s, 0, src[0])
        build(s, 1, src[1])
        for n in BLOCKS:
            for r in range(ROWS):
                if n == 0 and r + 2 < ROWS:
                    build(s, r + 2, src[r + 2])
                inner(acc, w, s, off, n, r, 0, EXT, True)
                if r in (2, 3):
                    finish(acc, bias, layer, r - 1, n, cx, h)

    @core_is(0)
    def _():
        work(h_in, acc_b, 256, 0)

    @core_is(1)
    def _():
        work(recv, acc_a, 0, 1)


def k_fourth(top, bot, w, bias, cx_in, h_in, a_in, b_in, acc_a, acc_b, cx, h, up, down, s):
    halo(s, top[...], bot[...])

    def work(acc, off, layer):
        for end in (0, 1):
            for n in BLOCKS:
                outer(acc, w, ((s, off),), n, end)
        for end in (0, 1):
            for n in BLOCKS:
                finish(acc, bias, layer, ENDS[end][0], n, cx, h)

    @core_is(0)
    def _():
        work(acc_b, 256, 0)

    @core_is(1)
    def _():
        work(acc_a, 0, 1)

    up[...] = h[0]
    down[...] = h[ROWS - 1]


def k_fifth(h, w, acc_in, acc, s):
    @core_is(1)
    def _():
        build_center(s, 0, h[0])
        build_center(s, 1, h[1])
        for n in BLOCKS:
            for r in range(ROWS):
                if n == 0 and r + 2 < ROWS:
                    build_center(s, r + 2, h[r + 2])
                inner(acc, w, s, 256, n, r, 0, COLS, False)


def halo_center(s, top, bot):
    build_center(s, 0, top.astype(f32) * inside("gy", -1))
    build_center(s, 1, bot.astype(f32) * inside("gy", 1))


def k_sixth(top, bot, w, acc_in, acc, out, s):
    @core_is(0)
    def _():
        out[0] = top[...]
        out[1] = bot[...]

    @core_is(1)
    def _():
        halo_center(s, top[...], bot[...])
        for end in (0, 1):
            for n in BLOCKS:
                outer(acc, w, ((s, 256),), n, end, COLS)


def k_seventh(recv, h, cx, w, bias, acc_in, acc, hv, cv, s):
    @core_is(0)
    def _():
        for r in range(ROWS):
            hv[r] = h[r].astype(f32)[PAD : PAD + COLS].astype(bf16)
            cv[r] = cx[r, PAD : PAD + COLS]

    @core_is(1)
    def _():
        build_center(s, 0, recv[0])
        build_center(s, 1, recv[1])
        for n in BLOCKS:
            for r in range(ROWS):
                if n == 0 and r + 2 < ROWS:
                    build_center(s, r + 2, recv[r + 2])
                inner(acc, w, s, 0, n, r, 0, COLS, True)
                if r in (2, 3):
                    finish_center(acc, bias, r - 1, n, cx, hv, cv)


def k_last(two, cx, w, bias, hv_in, cv_in, acc_in, acc, hv, cv, ho, co, s, sem):
    def out(r):
        return (
            pltpu.make_async_copy(hv.at[r], ho.at[0, r], sem.at[0, r]),
            pltpu.make_async_copy(cv.at[r], co.at[0, r], sem.at[1, r]),
        )

    def send(r):
        for c in out(r):
            c.start()

    for r in (1, 2):
        send(r)

    @core_is(1)
    def _():
        halo_center(s, two[0], two[1])
        for end in (0, 1):
            for n in BLOCKS:
                outer(acc, w, ((s, 0),), n, end, COLS)
        for end in (0, 1):
            for n in BLOCKS:
                finish_center(acc, bias, ENDS[end][0], n, cx, hv, cv)

    for r in (0, 3):
        send(r)
    for r in range(ROWS):
        for c in out(r):
            c.wait()


def both_ways(axis, to_low, to_high):
    n = lax.axis_size(axis)
    from_low = lax.ppermute(to_high, axis, [(i, (i + 1) % n) for i in range(n)])
    from_high = lax.ppermute(to_low, axis, [(i, (i - 1) % n) for i in range(n)])
    return from_low, from_high


def per_device(frames, hidden_init, cell_init, conv_weight, conv_bias):
    bias = conv_bias
    w_far = far(conv_weight[0].reshape(9, 512, GATES))
    frames_far, hidden_far, cell_far = far(frames), far(hidden_init), far(cell_init)
    swap = [(0, 1), (1, 0)]
    sums, tile, tile32, row = vm(ACC, f32), vm(TILE, bf16), vm(TILE, f32), vm((EXT, CH), bf16)

    edge = vm(EDGE, bf16)
    to_left, to_right = call(
        k_edges,
        [edge, edge],
        [frames_far, hidden_far, cell_far],
        far=(0, 1, 2),
        scratch=[
            pltpu.VMEM((2, 2, ROWS, 16, CH), bf16),
            pltpu.VMEM((2, ROWS, 16, CH), bf16),
            pltpu.VMEM((2, ROWS, 16, CH), f32),
            pltpu.SemaphoreType.DMA((6,)),
        ],
    )
    left, right = both_ways("gx", to_left, to_right)
    w, acc_a = call(
        k_hidden,
        [vm((9, 512, GATES), bf16), sums],
        [hidden_far, w_far],
        far=(0, 1),
        scratch=[pltpu.VMEM(STACK, bf16), pltpu.VMEM((ROWS, COLS, CH), bf16), pltpu.SemaphoreType.DMA((3, 2, 4))],
        part=0.4,
    )

    rows = vm((3, EXT, CH), bf16)
    to_up, to_down = call(k_rows, [rows, rows], [frames, hidden_init, left, right])
    top, bot = both_ways("gy", to_up, to_down)
    acc_a, acc_b, cx, h = call(
        k_frames,
        [sums, sums, tile32, tile],
        [frames, hidden_init, cell_init, w, bias, left, right, acc_a],
        aliases={7: 0},
        scratch=[pltpu.VMEM((2,) + STACK, bf16), pltpu.VMEM((3, ROWS, 32, CH), bf16)],
        part=0.95,
        limit=10,
    )
    acc_a, h, cx = call(
        k_first,
        [sums, tile, tile32],
        [top, bot, w, bias, cx, h, acc_a],
        aliases={4: 2, 5: 1, 6: 0},
        scratch=[pltpu.VMEM((2,) + PAIR, bf16)],
        part=0.3,
    )

    recv = lax.ppermute(h, "layer", swap)
    (acc_b,) = call(k_second, [sums], [top, bot, w, acc_b], aliases={3: 0}, scratch=[pltpu.VMEM(PAIR, bf16)], part=0.1)
    to_up, to_down = call(k_pick, [row, row], [h, recv])
    top, bot = both_ways("gy", to_up, to_down)
    acc_a, acc_b, cx, h = call(
        k_third,
        [sums, sums, tile32, tile],
        [h, recv, w, bias, cx, acc_a, acc_b],
        aliases={4: 2, 5: 0, 6: 1},
        scratch=[pltpu.VMEM(STACK, bf16)],
        part=0.45,
    )
    acc_a, acc_b, cx, h, to_up, to_down = call(
        k_fourth,
        [sums, sums, tile32, tile, row, row],
        [top, bot, w, bias, cx, h, acc_a, acc_b],
        aliases={4: 2, 5: 3, 6: 0, 7: 1},
        scratch=[pltpu.VMEM(PAIR, bf16)],
        part=0.3,
    )

    top, bot = both_ways("gy", to_up, to_down)
    recv = lax.ppermute(h, "layer", swap)
    center = pltpu.VMEM(CENTER, bf16)
    ends = pltpu.VMEM((3, 2, COLS, CH), bf16)
    (acc_b,) = call(k_fifth, [sums], [h, w, acc_b], aliases={2: 0}, scratch=[center], part=0.45)
    acc_b, two = call(
        k_sixth,
        [sums, vm((2, EXT, CH), bf16)],
        [top, bot, w, acc_b],
        aliases={3: 0},
        scratch=[ends],
        part=0.1,
    )
    two = lax.ppermute(two, "layer", swap)
    hv, cv = vm((ROWS, COLS, CH), bf16), vm((ROWS, COLS, CH), f32)
    acc_b, hid, cell = call(
        k_seventh, [sums, hv, cv], [recv, h, cx, w, bias, acc_b], aliases={5: 0}, scratch=[center], part=0.45
    )
    _, _, _, ho, co = call(
        k_last,
        [
            sums,
            hv,
            cv,
            jax.ShapeDtypeStruct((1, ROWS, COLS, CH), bf16),
            jax.ShapeDtypeStruct((1, ROWS, COLS, CH), f32),
        ],
        [two, cx, w, bias, hid, cell, acc_b],
        aliases={4: 1, 5: 2, 6: 0},
        far_out=(3, 4),
        scratch=[ends, pltpu.SemaphoreType.DMA((2, ROWS))],
        part=0.3,
    )
    return ho, co


def solution(mesh):
    placed = (
        P(None, "gy", "gx", None),
        P("layer", "gy", "gx", None),
        P("layer", "gy", "gx", None),
        P("layer", None, None),
        P(),
    )
    return jax.shard_map(
        per_device,
        mesh=mesh,
        in_specs=placed,
        out_specs=(P("layer", "gy", "gx", None), P("layer", "gy", "gx", None)),
        check_vma=False,
    )
```

```python
import jax
import jax.numpy as jnp
from jax import lax
from jax.experimental import pallas as pl
from jax.experimental.pallas import tpu as pltpu
from jax.sharding import PartitionSpec as P

f32 = jnp.float32
bf16 = jnp.bfloat16
ROWS, COLS, CH, GATES = 4, 256, 256, 1024
PAD = 8
EXT = COLS + 2 * PAD
LO, HI = 16, EXT - 16
NB = 512
UNIT = 2 * ROWS * COLS * 4608 * 1024
ACC = (ROWS, EXT, GATES)
TILE = (ROWS, EXT, CH)
STACK = (3, ROWS, EXT, CH)
PAIR = (3, 2, EXT, CH)
EDGE = (20, PAD, CH)

CENTER = (3, ROWS, COLS, CH)
GROUP = CH // 2

ANYV = pl.BlockSpec(memory_space=pltpu.VMEM)
HBM = pl.BlockSpec(memory_space=pltpu.HBM)


def vm(shape, dtype):
    return pltpu.VMEM(shape, dtype)


class Chain:
    def __init__(self):
        self.mark = ()

    def __call__(self, body, outs, args, aliases=None, scratch=(), part=0.0, limit=8, far=(), far_out=()):
        flat, tree = jax.tree.flatten(list(args))
        places = jax.tree.unflatten(tree, range(len(flat)))
        aliases = {places[i]: o for i, o in (aliases or {}).items()}
        given, marks, made = len(flat), len(self.mark), len(outs)

        def kernel(*refs):
            first = given + marks
            inputs = jax.tree.unflatten(tree, refs[:given])
            return body(*inputs, *refs[first : first + made], *refs[first + made + 1 :])

        *results, mark = pl.pallas_call(
            kernel,
            in_specs=[HBM if i in far else ANYV for i in range(given)] + [ANYV] * marks,
            out_specs=[HBM if i in far_out else ANYV for i in range(made)] + [ANYV],
            out_shape=list(outs) + [vm((8, 128), f32)],
            scratch_shapes=list(scratch),
            input_output_aliases=aliases,
            compiler_params=pltpu.CompilerParams(vmem_limit_bytes=limit << 20),
            cost_estimate=pl.CostEstimate(flops=int(UNIT * part), bytes_accessed=1 << 20, transcendentals=0),
        )(*flat, *self.mark)
        self.mark = (mark,)
        return results


def far(x):
    return pltpu.with_memory_space_constraint(x, pltpu.HBM)


def core_is(k):
    return pl.when(lax.axis_index("layer") == k)


def inside(axis, step):
    at = lax.axis_index(axis) + step
    return jnp.logical_and(at >= 0, at < lax.axis_size(axis)).astype(f32)


def build(stack, r, x):
    x = x.astype(f32)
    stack[0, r] = pltpu.roll(x, 1, 0).astype(bf16)
    stack[1, r] = x.astype(bf16)
    stack[2, r] = pltpu.roll(x, EXT - 1, 0).astype(bf16)


def widen(row, left, right):
    a = left.astype(f32) * inside("gx", -1)
    b = right.astype(f32) * inside("gx", 1)
    return jnp.concatenate([a, row.astype(f32), b], axis=0)


def bare(row):
    zero = jnp.zeros((PAD, CH), f32)
    return jnp.concatenate([zero, row.astype(f32), zero], axis=0)


def build_center(stack, r, x):
    x = x.astype(f32)
    for dx, y in ((0, pltpu.roll(x, 1, 0)), (1, x), (2, pltpu.roll(x, EXT - 1, 0))):
        stack[dx, r] = y[PAD : PAD + COLS].astype(bf16)


BLOCKS = range(GATES // NB)


def taps(w, n, lhs, off, tap, total):
    d = jnp.dot(lhs, w[tap, off : off + 256, n * NB : (n + 1) * NB], preferred_element_type=f32)
    return d if total is None else total + d


def inner(acc, w, stack, off, n, r, lo, hi, add):
    c = slice(n * NB, (n + 1) * NB)
    total = acc[r, lo:hi, c] if add else None
    for dy in range(3):
        q = r + dy - 1
        if 0 <= q < ROWS:
            for dx in range(3):
                total = taps(w, n, stack[dx, q, lo:hi, :], off, 3 * dy + dx, total)
    acc[r, lo:hi, c] = total


ENDS = ((0, 0, 0), (ROWS - 1, 1, 2))


def outer(acc, w, parts, n, end, m=EXT):
    r, q, dy = ENDS[end]
    c = slice(n * NB, (n + 1) * NB)
    total = acc[r, 0:m, c]
    for dx in range(3):
        for stack, off in parts:
            total = taps(w, n, stack[dx, q], off, 3 * dy + dx, total)
    acc[r, 0:m, c] = total


def sigmoid(x):
    return 0.5 * jnp.tanh(0.5 * x) + 0.5


def gates_at(acc, bias, layer, r, n, at, cell):
    def gate(i):
        b = bias[layer : layer + 1, i * CH + n * GROUP : i * CH + (n + 1) * GROUP]
        return acc[r, at, i * CH + n * GROUP : i * CH + (n + 1) * GROUP] + b

    cell = sigmoid(gate(1)) * cell + sigmoid(gate(0)) * jnp.tanh(gate(3))
    return cell, sigmoid(gate(2)) * jnp.tanh(cell)


def finish(acc, bias, layer, r, n, cx, h):
    ch = slice(n * GROUP, (n + 1) * GROUP)
    for k in range(EXT // 16):
        at = slice(k * 16, (k + 1) * 16)
        new, hid = gates_at(acc, bias, layer, r, n, at, cx[r, at, ch])
        cx[r, at, ch] = new
        if k in (0, EXT // 16 - 1):
            half = lax.broadcasted_iota(jnp.int32, (16, GROUP), 0) < PAD
            kept = half if k else jnp.logical_not(half)
            hid = hid * jnp.where(kept, 1.0, inside("gx", 1 if k else -1))
        h[r, at, ch] = hid.astype(bf16)


def ends(acc, w, parts, bias, layer, cx, h):
    for n in BLOCKS:
        outer(acc, w, parts, n, 0)
    for n in BLOCKS:
        outer(acc, w, parts, n, 1)
        finish(acc, bias, layer, 0, n, cx, h)
    for n in BLOCKS:
        finish(acc, bias, layer, ROWS - 1, n, cx, h)


def finish_center(acc, bias, r, n, cx, hv, cv):
    ch = slice(n * GROUP, (n + 1) * GROUP)
    for k in range(COLS // 16):
        at = slice(k * 16, (k + 1) * 16)
        src = slice(k * 16 + PAD, (k + 1) * 16 + PAD)
        new, hid = gates_at(acc, bias, 1, r, n, at, cx[r, src, ch])
        cv[r, at, ch] = new
        hv[r, at, ch] = hid.astype(bf16)


def k_edges(fr, hid, cell, to_left, to_right, fs, hs, cs, sem):
    jobs = []
    for side, a in ((0, 0), (1, COLS - 16)):
        jobs.append((fr.at[:, :, a : a + 16, :], fs.at[side]))
        jobs.append((hid.at[0, :, a : a + 16, :], hs.at[side]))
        jobs.append((cell.at[0, :, a : a + 16, :], cs.at[side]))
    copies = [pltpu.make_async_copy(src, dst, sem.at[i]) for i, (src, dst) in enumerate(jobs)]
    for c in copies:
        c.start()
    for c in copies:
        c.wait()
    for side, out, at in ((0, to_left, slice(0, PAD)), (1, to_right, slice(PAD, 16))):
        for r in range(ROWS):
            out[r] = fs[side, 0, r, at]
            out[4 + r] = fs[side, 1, r, at]
            out[8 + r] = hs[side, r, at]
            c = cs[side, r, at]
            hi = c.astype(bf16)
            out[12 + r] = hi
            out[16 + r] = (c - hi.astype(f32)).astype(bf16)


def k_hidden(hid, w, acc, s):
    build(s, 0, bare(hid[0, 0]))
    build(s, 1, bare(hid[0, 1]))
    for n in BLOCKS:
        for r in range(ROWS):
            if n == 0 and r + 2 < ROWS:
                build(s, r + 2, bare(hid[0, r + 2]))
            inner(acc, w, s, 256, n, r, LO, HI, False)


def below():
    return lax.rem(lax.axis_index("layer") + lax.axis_index("gy"), 2) == 0


def my_row():
    return jnp.where(below(), ROWS - 1, 0)


def halo(s, mine, other, make=None):
    make = make or build
    mine, other = mine.astype(f32), other.astype(f32)
    make(s, 0, jnp.where(below(), other, mine) * inside("gy", -1))
    make(s, 1, jnp.where(below(), mine, other) * inside("gy", 1))


def k_lend(hid, left, right, out):
    r = ROWS - 1 - my_row()
    out[...] = widen(hid[0, r], left[8 + r], right[8 + r]).astype(bf16)


def k_rows(fr, hid, left, right, lent, out, later):
    r = my_row()
    own = widen(hid[0, r], left[8 + r], right[8 + r])
    lent = lent[...].astype(f32)
    first = lax.axis_index("layer") == 0
    out[0] = widen(fr[0, r], left[r], right[r]).astype(bf16)
    out[1] = jnp.where(first, own, lent).astype(bf16)
    later[0] = widen(fr[1, r], left[4 + r], right[4 + r]).astype(bf16)
    later[1] = jnp.where(first, lent, own).astype(bf16)


def k_sides(hid, cell, w, left, right, acc_in, acc, cx, t):
    for r in range(ROWS):
        a = left[12 + r].astype(f32) + left[16 + r].astype(f32)
        b = right[12 + r].astype(f32) + right[16 + r].astype(f32)
        cx[r] = jnp.concatenate([a, cell[0, r], b], axis=0)
        x = widen(hid[0, r], left[8 + r], right[8 + r])
        for dx, y in ((0, pltpu.roll(x, 1, 0)), (1, x), (2, pltpu.roll(x, EXT - 1, 0))):
            t[dx, r, 0:16] = y[0:16].astype(bf16)
            t[dx, r, 16:32] = y[HI:EXT].astype(bf16)
    for n in BLOCKS:
        c = slice(n * NB, (n + 1) * NB)
        total = None
        for dy in range(3):
            m = ROWS if dy == 1 else ROWS - 1
            first = max(dy - 1, 0)
            for dx in range(3):
                lhs = t[dx, first : first + m].reshape(m * 32, CH)
                d = taps(w, n, lhs, 256, 3 * dy + dx, None)
                zero = jnp.zeros((32, NB), f32)
                if dy == 0:
                    d = jnp.concatenate([zero, d], axis=0)
                if dy == 2:
                    d = jnp.concatenate([d, zero], axis=0)
                total = d if total is None else total + d
        for r in range(ROWS):
            acc[r, 0:LO, c] = total[r * 32 : r * 32 + 16]
            acc[r, HI:EXT, c] = total[r * 32 + 16 : r * 32 + 32]


def k_frame(fr, w, left, right, acc_in, acc, s1, s):
    @core_is(0)
    def _():
        def frame(dst, i, r):
            build(dst, r, widen(fr[i, r], left[4 * i + r], right[4 * i + r]))

        frame(s, 0, 0)
        frame(s, 0, 1)
        for n in BLOCKS:
            for r in range(ROWS):
                if n == 0 and r + 2 < ROWS:
                    frame(s, 0, r + 2)
                inner(acc, w, s, 0, n, r, 0, EXT, True)
                if n == 1:
                    frame(s1, 1, r)


def k_next(s1, w, bias, acc_in, cx_in, acc_b, cx, h):
    @core_is(0)
    def _():
        for r in range(ROWS):
            inner(acc_b, w, s1, 0, 0, r, 0, EXT, False)
            finish(acc_in, bias, 0, 1 + r // 2, r % 2, cx, h)


def k_rest(s1, w, b_in, acc_b):
    @core_is(0)
    def _():
        for r in range(ROWS):
            inner(acc_b, w, s1, 0, 1, r, 0, EXT, False)


def k_first(mine, other, w, bias, cx_in, h_in, acc_in, acc, h, cx, s):
    @core_is(0)
    def _():
        halo(s.at[0], mine[0], other[0])
        halo(s.at[1], mine[1], other[1])
        ends(acc, w, ((s.at[0], 0), (s.at[1], 256)), bias, 0, cx, h)


def k_second(mine, other, w, a_in, b_in, acc_a, acc_b, s):
    def work(i, acc, off):
        halo(s, mine[i], other[i])
        for end in (0, 1):
            for n in BLOCKS:
                outer(acc, w, ((s, off),), n, end)

    @core_is(0)
    def _():
        work(0, acc_b, 0)

    @core_is(1)
    def _():
        work(1, acc_a, 256)


def k_pick(h, recv, out):
    r = my_row()

    @core_is(0)
    def _():
        out[...] = h[r]

    @core_is(1)
    def _():
        out[...] = recv[r]


def k_third(h_in, recv, w, bias, cx_in, a_in, b_in, acc_a, acc_b, cx, h, s):
    def work(src, acc, off, layer):
        build(s, 0, src[0])
        build(s, 1, src[1])
        for r in (1, 2):
            build(s, r + 1, src[r + 1])
            for n in BLOCKS:
                inner(acc, w, s, off, n, r, 0, EXT, True)
                if r == 2:
                    finish(acc, bias, layer, 1, n, cx, h)
        for n in BLOCKS:
            finish(acc, bias, layer, 2, n, cx, h)

    @core_is(0)
    def _():
        work(h_in, acc_b, 256, 0)

    @core_is(1)
    def _():
        work(recv, acc_a, 0, 1)


def k_ends(w, s, a_in, b_in, acc_a, acc_b):
    def work(acc, off):
        for n in BLOCKS:
            for r in (0, ROWS - 1):
                inner(acc, w, s, off, n, r, 0, EXT, True)

    @core_is(0)
    def _():
        work(acc_b, 256)

    @core_is(1)
    def _():
        work(acc_a, 0)


def k_nothing(x_in, x):
    pass


def k_fourth(mine, other, w, bias, cx_in, h_in, a_in, b_in, acc_a, acc_b, cx, h, out, s):
    halo(s, mine[...], other[...])

    def work(acc, off, layer):
        ends(acc, w, ((s, off),), bias, layer, cx, h)

    @core_is(0)
    def _():
        work(acc_b, 256, 0)

    @core_is(1)
    def _():
        work(acc_a, 0, 1)

    out[...] = h[my_row()]


def k_fifth(h, w, acc_in, acc, s):
    @core_is(1)
    def _():
        build_center(s, 0, h[0])
        build_center(s, 1, h[1])
        for r in range(ROWS):
            if r + 2 < ROWS:
                build_center(s, r + 2, h[r + 2])
            inner(acc, w, s, 256, 0, r, 0, COLS, False)


def k_lent(recv, out):
    out[...] = recv[my_row()]


def k_join(own, lent, out):
    core = lax.axis_index("layer")
    out[core] = own[...]
    out[1 - core] = lent[...]


def k_sixth(recv, w, s1, acc_in, acc, s):
    @core_is(1)
    def _():
        for r in range(ROWS):
            inner(acc, w, s1, 256, 1, r, 0, COLS, False)
            build_center(s, r, recv[r])
        for r in range(ROWS):
            inner(acc, w, s, 0, 0, r, 0, COLS, True)


def k_seventh(h, cx, w, bias, s, acc_in, acc, hv, cv):
    @core_is(0)
    def _():
        for r in range(ROWS):
            hv[r] = h[r].astype(f32)[PAD : PAD + COLS].astype(bf16)
            cv[r] = cx[r, PAD : PAD + COLS]

    @core_is(1)
    def _():
        for r, done in ((1, None), (2, 1), (0, 2), (3, None)):
            inner(acc, w, s, 0, 1, r, 0, COLS, True)
            if done:
                for n in BLOCKS:
                    finish_center(acc, bias, done, n, cx, hv, cv)


def k_last(mine, other, cx, w, bias, hv_in, cv_in, acc_in, acc, hv, cv, ho, co, s, sem):
    def out(r):
        return (
            pltpu.make_async_copy(hv.at[r], ho.at[0, r], sem.at[0, r]),
            pltpu.make_async_copy(cv.at[r], co.at[0, r], sem.at[1, r]),
        )

    def send(r):
        for c in out(r):
            c.start()

    for r in (1, 2):
        send(r)

    @core_is(1)
    def _():
        halo(s.at[0], mine[0], other[0], build_center)
        halo(s.at[1], mine[1], other[1], build_center)
        for end in (0, 1):
            for n in BLOCKS:
                outer(acc, w, ((s.at[0], 0), (s.at[1], 256)), n, end, COLS)
                if end:
                    finish_center(acc, bias, 0, n, cx, hv, cv)
        send(0)
        for n in BLOCKS:
            finish_center(acc, bias, ROWS - 1, n, cx, hv, cv)
        send(ROWS - 1)

    @core_is(0)
    def _():
        for r in (0, 3):
            send(r)

    for r in range(ROWS):
        for c in out(r):
            c.wait()


def swap_rows(x):
    ny, nx = lax.axis_size("gy"), lax.axis_size("gx")
    pairs = []
    for core in range(2):
        for y in range(ny):
            to = (y + 1 if (core + y) % 2 == 0 else y - 1) % ny
            pairs += [((core * ny + y) * nx + x, (core * ny + to) * nx + x) for x in range(nx)]
    return lax.ppermute(x, ("layer", "gy", "gx"), pairs)


def both_ways(axis, to_low, to_high):
    n = lax.axis_size(axis)
    from_low = lax.ppermute(to_high, axis, [(i, (i + 1) % n) for i in range(n)])
    from_high = lax.ppermute(to_low, axis, [(i, (i - 1) % n) for i in range(n)])
    return from_low, from_high


def per_device(frames, hidden_init, cell_init, conv_weight, conv_bias):
    call = Chain()
    bias = conv_bias
    frames_far, hidden_far, cell_far = far(frames), far(hidden_init), far(cell_init)
    swap = [(0, 1), (1, 0)]
    sums, tile, tile32, row = vm(ACC, f32), vm(TILE, bf16), vm(TILE, f32), vm((EXT, CH), bf16)

    edge = vm(EDGE, bf16)
    to_left, to_right = call(
        k_edges,
        [edge, edge],
        [frames_far, hidden_far, cell_far],
        far=(0, 1, 2),
        scratch=[
            pltpu.VMEM((2, 2, ROWS, 16, CH), bf16),
            pltpu.VMEM((2, ROWS, 16, CH), bf16),
            pltpu.VMEM((2, ROWS, 16, CH), f32),
            pltpu.SemaphoreType.DMA((6,)),
        ],
        part=2.0,
    )
    left, right = both_ways("gx", to_left, to_right)
    w = pltpu.with_memory_space_constraint(conv_weight[0].reshape(9, 512, GATES), pltpu.VMEM)
    (acc_a,) = call(k_hidden, [sums], [hidden_init, w], scratch=[pltpu.VMEM(STACK, bf16)], part=0.4)

    def swap_cores(x):
        return lax.ppermute(x, "layer", swap)

    def hold(x):
        return call(k_nothing, [vm(x.shape, x.dtype)], [x], aliases={0: 0})[0]

    lent = swap_cores(call(k_lend, [row], [hidden_init, left, right])[0])
    acc_a, cx = call(
        k_sides,
        [sums, tile32],
        [hidden_init, cell_init, w, left, right, acc_a],
        aliases={5: 0},
        scratch=[pltpu.VMEM((3, ROWS, 32, CH), bf16)],
        part=0.1,
    )
    two_rows = vm((2, EXT, CH), bf16)
    rows, later = call(k_rows, [two_rows, two_rows], [frames, hidden_init, left, right, lent])
    mine, mine_later = swap_rows(rows), swap_rows(later)
    stack = vm(STACK, bf16)
    acc_a, next_stack = call(
        k_frame,
        [sums, stack],
        [frames, w, left, right, acc_a],
        aliases={4: 0},
        scratch=[pltpu.VMEM(STACK, bf16)],
        part=0.45,
    )
    acc_b, cx, h = call(k_next, [sums, tile32, tile], [next_stack, w, bias, acc_a, cx], aliases={4: 1}, part=0.22)
    mine = hold(mine)
    other = swap_cores(mine)
    (acc_b,) = call(k_rest, [sums], [next_stack, w, acc_b], aliases={2: 0}, part=0.22)
    mine_later = hold(mine_later)
    other_later = swap_cores(mine_later)
    acc_a, h, cx = call(
        k_first,
        [sums, tile, tile32],
        [mine, other, w, bias, cx, h, acc_a],
        aliases={4: 2, 5: 1, 6: 0},
        scratch=[pltpu.VMEM((2,) + PAIR, bf16)],
        part=0.3,
    )

    recv = swap_cores(h)
    acc_a, acc_b = call(
        k_second,
        [sums, sums],
        [mine_later, other_later, w, acc_a, acc_b],
        aliases={3: 0, 4: 1},
        scratch=[pltpu.VMEM(PAIR, bf16)],
        part=0.5,
    )
    mine = swap_rows(call(k_pick, [row], [h, recv])[0])
    acc_a, acc_b, cx, h2, s = call(
        k_third,
        [sums, sums, tile32, tile, stack],
        [h, recv, w, bias, cx, acc_a, acc_b],
        aliases={4: 2, 5: 0, 6: 1},
        part=0.25,
    )
    mine = hold(mine)
    other = swap_cores(mine)
    acc_a, acc_b = call(k_ends, [sums, sums], [w, s, acc_a, acc_b], aliases={2: 0, 3: 1}, part=0.2)
    acc_a, acc_b, cx, h, out = call(
        k_fourth,
        [sums, sums, tile32, tile, row],
        [mine, other, w, bias, cx, h2, acc_a, acc_b],
        aliases={4: 2, 5: 3, 6: 0, 7: 1},
        scratch=[pltpu.VMEM(PAIR, bf16)],
        part=0.2,
    )

    recv = swap_cores(h)
    mine = swap_rows(out)
    acc_b, s = call(k_fifth, [sums, vm(CENTER, bf16)], [h, w, acc_b], aliases={2: 0}, part=0.22)
    mine_lent = swap_rows(call(k_lent, [row], [recv])[0])
    hv, cv = vm((ROWS, COLS, CH), bf16), vm((ROWS, COLS, CH), f32)
    acc_b, s = call(k_sixth, [sums, vm(CENTER, bf16)], [recv, w, s, acc_b], aliases={3: 0}, part=0.45)
    (mine,) = call(k_join, [two_rows], [mine, mine_lent])
    other = swap_cores(mine)
    acc_b, hid, cell = call(k_seventh, [sums, hv, cv], [h, cx, w, bias, s, acc_b], aliases={5: 0}, part=0.25)
    _, _, _, ho, co = call(
        k_last,
        [
            sums,
            hv,
            cv,
            jax.ShapeDtypeStruct((1, ROWS, COLS, CH), bf16),
            jax.ShapeDtypeStruct((1, ROWS, COLS, CH), f32),
        ],
        [mine, other, cx, w, bias, hid, cell, acc_b],
        aliases={5: 1, 6: 2, 7: 0},
        far_out=(3, 4),
        scratch=[pltpu.VMEM((2, 3, 2, COLS, CH), bf16), pltpu.SemaphoreType.DMA((2, ROWS))],
        part=0.3,
    )
    return ho, co


def solution(mesh):
    placed = (
        P(None, "gy", "gx", None),
        P("layer", "gy", "gx", None),
        P("layer", "gy", "gx", None),
        P("layer", None, None),
        P(),
    )
    return jax.shard_map(
        per_device,
        mesh=mesh,
        in_specs=placed,
        out_specs=(P("layer", "gy", "gx", None), P("layer", "gy", "gx", None)),
        check_vma=False,
    )
```

```python
import jax
import jax.numpy as jnp
from jax import lax
from jax.experimental import pallas as pl
from jax.experimental.pallas import tpu as pltpu
from jax.sharding import PartitionSpec as P

f32 = jnp.float32
bf16 = jnp.bfloat16
ROWS, COLS, CH, GATES = 4, 256, 256, 1024
PAD = 8
EXT = COLS + 2 * PAD
LO, HI = 16, EXT - 16
NB = 512
UNIT = 2 * ROWS * COLS * 4608 * 1024
ACC = (ROWS, EXT, GATES)
TILE = (ROWS, EXT, CH)
STACK = (3, ROWS, EXT, CH)
PAIR = (3, 2, EXT, CH)
EDGE = (20, PAD, CH)

CENTER = (3, ROWS, COLS, CH)
GROUP = CH // 2

ANYV = pl.BlockSpec(memory_space=pltpu.VMEM)
HBM = pl.BlockSpec(memory_space=pltpu.HBM)


def vm(shape, dtype):
    return pltpu.VMEM(shape, dtype)


class Chain:
    def __init__(self):
        self.mark = ()

    def __call__(self, body, outs, args, aliases=None, scratch=(), part=0.0, limit=8, far=(), far_out=()):
        flat, tree = jax.tree.flatten(list(args))
        places = jax.tree.unflatten(tree, range(len(flat)))
        aliases = {places[i]: o for i, o in (aliases or {}).items()}
        given, marks, made = len(flat), len(self.mark), len(outs)

        def kernel(*refs):
            first = given + marks
            inputs = jax.tree.unflatten(tree, refs[:given])
            return body(*inputs, *refs[first : first + made], *refs[first + made + 1 :])

        *results, mark = pl.pallas_call(
            kernel,
            in_specs=[HBM if i in far else ANYV for i in range(given)] + [ANYV] * marks,
            out_specs=[HBM if i in far_out else ANYV for i in range(made)] + [ANYV],
            out_shape=list(outs) + [vm((8, 128), f32)],
            scratch_shapes=list(scratch),
            input_output_aliases=aliases,
            compiler_params=pltpu.CompilerParams(vmem_limit_bytes=limit << 20),
            cost_estimate=pl.CostEstimate(flops=int(UNIT * part), bytes_accessed=1 << 20, transcendentals=0),
        )(*flat, *self.mark)
        self.mark = (mark,)
        return results


def far(x):
    return pltpu.with_memory_space_constraint(x, pltpu.HBM)


def core_is(k):
    return pl.when(lax.axis_index("layer") == k)


def inside(axis, step):
    at = lax.axis_index(axis) + step
    return jnp.logical_and(at >= 0, at < lax.axis_size(axis)).astype(f32)


def build(stack, r, x):
    x = x.astype(f32)
    stack[0, r] = pltpu.roll(x, 1, 0).astype(bf16)
    stack[1, r] = x.astype(bf16)
    stack[2, r] = pltpu.roll(x, EXT - 1, 0).astype(bf16)


def widen(row, left, right):
    a = left.astype(f32) * inside("gx", -1)
    b = right.astype(f32) * inside("gx", 1)
    return jnp.concatenate([a, row.astype(f32), b], axis=0)


def bare(row):
    zero = jnp.zeros((PAD, CH), f32)
    return jnp.concatenate([zero, row.astype(f32), zero], axis=0)


def build_center(stack, r, x):
    x = x.astype(f32)
    for dx, y in ((0, pltpu.roll(x, 1, 0)), (1, x), (2, pltpu.roll(x, EXT - 1, 0))):
        stack[dx, r] = y[PAD : PAD + COLS].astype(bf16)


BLOCKS = range(GATES // NB)


def taps(w, n, lhs, off, tap, total):
    d = jnp.dot(lhs, w[tap, off : off + 256, n * NB : (n + 1) * NB], preferred_element_type=f32)
    return d if total is None else total + d


def inner(acc, w, stack, off, n, r, lo, hi, add):
    c = slice(n * NB, (n + 1) * NB)
    total = acc[r, lo:hi, c] if add else None
    for dy in range(3):
        q = r + dy - 1
        if 0 <= q < ROWS:
            for dx in range(3):
                total = taps(w, n, stack[dx, q, lo:hi, :], off, 3 * dy + dx, total)
    acc[r, lo:hi, c] = total


ENDS = ((0, 0, 0), (ROWS - 1, 1, 2))


def outer(acc, w, parts, n, end, m=EXT):
    r, q, dy = ENDS[end]
    c = slice(n * NB, (n + 1) * NB)
    total = acc[r, 0:m, c]
    for dx in range(3):
        for stack, off in parts:
            total = taps(w, n, stack[dx, q], off, 3 * dy + dx, total)
    acc[r, 0:m, c] = total


def sigmoid(x):
    return 0.5 * jnp.tanh(0.5 * x) + 0.5


def gates_at(acc, bias, layer, r, n, at, cell):
    def gate(i):
        b = bias[layer : layer + 1, i * CH + n * GROUP : i * CH + (n + 1) * GROUP]
        return acc[r, at, i * CH + n * GROUP : i * CH + (n + 1) * GROUP] + b

    cell = sigmoid(gate(1)) * cell + sigmoid(gate(0)) * jnp.tanh(gate(3))
    return cell, sigmoid(gate(2)) * jnp.tanh(cell)


def finish(acc, bias, layer, r, n, cx, h):
    ch = slice(n * GROUP, (n + 1) * GROUP)
    for k in range(EXT // 16):
        at = slice(k * 16, (k + 1) * 16)
        new, hid = gates_at(acc, bias, layer, r, n, at, cx[r, at, ch])
        cx[r, at, ch] = new
        if k in (0, EXT // 16 - 1):
            half = lax.broadcasted_iota(jnp.int32, (16, GROUP), 0) < PAD
            kept = half if k else jnp.logical_not(half)
            hid = hid * jnp.where(kept, 1.0, inside("gx", 1 if k else -1))
        h[r, at, ch] = hid.astype(bf16)


def ends(acc, w, parts, bias, layer, cx, h):
    for n in BLOCKS:
        outer(acc, w, parts, n, 0)
    for n in BLOCKS:
        outer(acc, w, parts, n, 1)
        finish(acc, bias, layer, 0, n, cx, h)
    for n in BLOCKS:
        finish(acc, bias, layer, ROWS - 1, n, cx, h)


def finish_center(acc, bias, r, n, cx, hv, cv):
    ch = slice(n * GROUP, (n + 1) * GROUP)
    for k in range(COLS // 16):
        at = slice(k * 16, (k + 1) * 16)
        src = slice(k * 16 + PAD, (k + 1) * 16 + PAD)
        new, hid = gates_at(acc, bias, 1, r, n, at, cx[r, src, ch])
        cv[0, r, at, ch] = new
        hv[0, r, at, ch] = hid.astype(bf16)


def k_edges(fr, hid, cell, to_left, to_right, fs, hs, cs, sem):
    jobs = []
    for side, a in ((0, 0), (1, COLS - 16)):
        jobs.append((fr.at[:, :, a : a + 16, :], fs.at[side]))
        jobs.append((hid.at[0, :, a : a + 16, :], hs.at[side]))
        jobs.append((cell.at[0, :, a : a + 16, :], cs.at[side]))
    copies = [pltpu.make_async_copy(src, dst, sem.at[i]) for i, (src, dst) in enumerate(jobs)]
    for c in copies:
        c.start()
    for c in copies:
        c.wait()
    for side, out, at in ((0, to_left, slice(0, PAD)), (1, to_right, slice(PAD, 16))):
        for r in range(ROWS):
            out[r] = fs[side, 0, r, at]
            out[4 + r] = fs[side, 1, r, at]
            out[8 + r] = hs[side, r, at]
            c = cs[side, r, at]
            hi = c.astype(bf16)
            out[12 + r] = hi
            out[16 + r] = (c - hi.astype(f32)).astype(bf16)


def k_hidden(hid, w, acc, s):
    build(s, 0, bare(hid[0, 0]))
    build(s, 1, bare(hid[0, 1]))
    for n in BLOCKS:
        for r in range(ROWS):
            if n == 0 and r + 2 < ROWS:
                build(s, r + 2, bare(hid[0, r + 2]))
            inner(acc, w, s, 256, n, r, LO, HI, False)


def below():
    return lax.rem(lax.axis_index("layer") + lax.axis_index("gy"), 2) == 0


def my_row():
    return jnp.where(below(), ROWS - 1, 0)


def halo(s, mine, other, make=None):
    make = make or build
    mine, other = mine.astype(f32), other.astype(f32)
    make(s, 0, jnp.where(below(), other, mine) * inside("gy", -1))
    make(s, 1, jnp.where(below(), mine, other) * inside("gy", 1))


def k_lend(hid, left, right, out):
    r = ROWS - 1 - my_row()
    out[...] = widen(hid[0, r], left[8 + r], right[8 + r]).astype(bf16)


def k_rows(fr, hid, left, right, lent, out, later):
    r = my_row()
    own = widen(hid[0, r], left[8 + r], right[8 + r])
    lent = lent[...].astype(f32)
    first = lax.axis_index("layer") == 0
    out[0] = widen(fr[0, r], left[r], right[r]).astype(bf16)
    out[1] = jnp.where(first, own, lent).astype(bf16)
    later[0] = widen(fr[1, r], left[4 + r], right[4 + r]).astype(bf16)
    later[1] = jnp.where(first, lent, own).astype(bf16)


def k_sides(hid, cell, w, left, right, acc_in, acc, cx, t):
    for r in range(ROWS):
        a = left[12 + r].astype(f32) + left[16 + r].astype(f32)
        b = right[12 + r].astype(f32) + right[16 + r].astype(f32)
        cx[r] = jnp.concatenate([a, cell[0, r], b], axis=0)
        x = widen(hid[0, r], left[8 + r], right[8 + r])
        for dx, y in ((0, pltpu.roll(x, 1, 0)), (1, x), (2, pltpu.roll(x, EXT - 1, 0))):
            t[dx, r, 0:16] = y[0:16].astype(bf16)
            t[dx, r, 16:32] = y[HI:EXT].astype(bf16)
    for n in BLOCKS:
        c = slice(n * NB, (n + 1) * NB)
        total = None
        for dy in range(3):
            m = ROWS if dy == 1 else ROWS - 1
            first = max(dy - 1, 0)
            for dx in range(3):
                lhs = t[dx, first : first + m].reshape(m * 32, CH)
                d = taps(w, n, lhs, 256, 3 * dy + dx, None)
                zero = jnp.zeros((32, NB), f32)
                if dy == 0:
                    d = jnp.concatenate([zero, d], axis=0)
                if dy == 2:
                    d = jnp.concatenate([d, zero], axis=0)
                total = d if total is None else total + d
        for r in range(ROWS):
            acc[r, 0:LO, c] = total[r * 32 : r * 32 + 16]
            acc[r, HI:EXT, c] = total[r * 32 + 16 : r * 32 + 32]


def k_frame(fr, w, left, right, acc_in, acc, s1, s):
    @core_is(0)
    def _():
        def frame(dst, i, r):
            build(dst, r, widen(fr[i, r], left[4 * i + r], right[4 * i + r]))

        frame(s, 0, 0)
        frame(s, 0, 1)
        for n in BLOCKS:
            for r in range(ROWS):
                if n == 0 and r + 2 < ROWS:
                    frame(s, 0, r + 2)
                inner(acc, w, s, 0, n, r, 0, EXT, True)
                if n == 1:
                    frame(s1, 1, r)


def k_next(s1, w, bias, acc_in, cx_in, acc_b, cx, h):
    @core_is(0)
    def _():
        for r in range(ROWS):
            inner(acc_b, w, s1, 0, 0, r, 0, EXT, False)
            finish(acc_in, bias, 0, 1 + r // 2, r % 2, cx, h)


def k_rest(s1, w, b_in, acc_b):
    @core_is(0)
    def _():
        for r in range(ROWS):
            inner(acc_b, w, s1, 0, 1, r, 0, EXT, False)


def k_first(mine, other, w, bias, cx_in, h_in, acc_in, acc, h, cx, s):
    @core_is(0)
    def _():
        halo(s.at[0], mine[0], other[0])
        halo(s.at[1], mine[1], other[1])
        ends(acc, w, ((s.at[0], 0), (s.at[1], 256)), bias, 0, cx, h)


def k_second(mine, other, w, a_in, b_in, acc_a, acc_b, s):
    def work(i, acc, off):
        halo(s, mine[i], other[i])
        for end in (0, 1):
            for n in BLOCKS:
                outer(acc, w, ((s, off),), n, end)

    @core_is(0)
    def _():
        work(0, acc_b, 0)

    @core_is(1)
    def _():
        work(1, acc_a, 256)


def k_pick(h, recv, out):
    r = my_row()

    @core_is(0)
    def _():
        out[...] = h[r]

    @core_is(1)
    def _():
        out[...] = recv[r]


def k_third(h_in, recv, w, bias, cx_in, a_in, b_in, acc_a, acc_b, cx, h, s):
    def work(src, acc, off, layer):
        build(s, 0, src[0])
        build(s, 1, src[1])
        for r in (1, 2):
            build(s, r + 1, src[r + 1])
            for n in BLOCKS:
                inner(acc, w, s, off, n, r, 0, EXT, True)
                if r == 2:
                    finish(acc, bias, layer, 1, n, cx, h)
        for n in BLOCKS:
            finish(acc, bias, layer, 2, n, cx, h)

    @core_is(0)
    def _():
        work(h_in, acc_b, 256, 0)

    @core_is(1)
    def _():
        work(recv, acc_a, 0, 1)


def k_ends(w, s, a_in, b_in, acc_a, acc_b):
    def work(acc, off):
        for n in BLOCKS:
            for r in (0, ROWS - 1):
                inner(acc, w, s, off, n, r, 0, EXT, True)

    @core_is(0)
    def _():
        work(acc_b, 256)

    @core_is(1)
    def _():
        work(acc_a, 0)


def k_nothing(x_in, x):
    pass


def k_fourth(mine, other, w, bias, cx_in, h_in, a_in, b_in, acc_a, acc_b, cx, h, out, s):
    halo(s, mine[...], other[...])

    def work(acc, off, layer):
        ends(acc, w, ((s, off),), bias, layer, cx, h)

    @core_is(0)
    def _():
        work(acc_b, 256, 0)

    @core_is(1)
    def _():
        work(acc_a, 0, 1)

    out[...] = h[my_row()]


def k_fifth(h, w, acc_in, acc, s):
    @core_is(1)
    def _():
        build_center(s, 0, h[0])
        build_center(s, 1, h[1])
        for r in range(ROWS):
            if r + 2 < ROWS:
                build_center(s, r + 2, h[r + 2])
            inner(acc, w, s, 256, 0, r, 0, COLS, False)


def k_lent(recv, out):
    out[...] = recv[my_row()]


def k_join(own, lent, out):
    core = lax.axis_index("layer")
    out[core] = own[...]
    out[1 - core] = lent[...]


def k_sixth(recv, w, s1, acc_in, acc, s):
    @core_is(1)
    def _():
        for r in range(ROWS):
            inner(acc, w, s1, 256, 1, r, 0, COLS, False)
            build_center(s, r, recv[r])
        for r in range(ROWS):
            inner(acc, w, s, 0, 0, r, 0, COLS, True)


def k_seventh(h, cx, w, bias, s, acc_in, acc, hv, cv):
    @core_is(0)
    def _():
        for r in range(ROWS):
            hv[0, r] = h[r].astype(f32)[PAD : PAD + COLS].astype(bf16)
            cv[0, r] = cx[r, PAD : PAD + COLS]

    @core_is(1)
    def _():
        for r, done in ((1, None), (2, 1), (0, 2), (3, None)):
            inner(acc, w, s, 0, 1, r, 0, COLS, True)
            if done:
                for n in BLOCKS:
                    finish_center(acc, bias, done, n, cx, hv, cv)


def k_last(mine, other, cx, w, bias, hv_in, cv_in, acc_in, acc, hv, cv, s):
    @core_is(1)
    def _():
        halo(s.at[0], mine[0], other[0], build_center)
        halo(s.at[1], mine[1], other[1], build_center)
        for end in (0, 1):
            for n in BLOCKS:
                outer(acc, w, ((s.at[0], 0), (s.at[1], 256)), n, end, COLS)
                if end:
                    finish_center(acc, bias, 0, n, cx, hv, cv)
        for n in BLOCKS:
            finish_center(acc, bias, ROWS - 1, n, cx, hv, cv)


def swap_rows(x):
    ny, nx = lax.axis_size("gy"), lax.axis_size("gx")
    pairs = []
    for core in range(2):
        for y in range(ny):
            to = (y + 1 if (core + y) % 2 == 0 else y - 1) % ny
            pairs += [((core * ny + y) * nx + x, (core * ny + to) * nx + x) for x in range(nx)]
    return lax.ppermute(x, ("layer", "gy", "gx"), pairs)


def both_ways(axis, to_low, to_high):
    n = lax.axis_size(axis)
    from_low = lax.ppermute(to_high, axis, [(i, (i + 1) % n) for i in range(n)])
    from_high = lax.ppermute(to_low, axis, [(i, (i - 1) % n) for i in range(n)])
    return from_low, from_high


def per_device(frames, hidden_init, cell_init, conv_weight, conv_bias):
    call = Chain()
    bias = conv_bias
    frames_far, hidden_far, cell_far = far(frames), far(hidden_init), far(cell_init)
    swap = [(0, 1), (1, 0)]
    sums, tile, tile32, row = vm(ACC, f32), vm(TILE, bf16), vm(TILE, f32), vm((EXT, CH), bf16)

    edge = vm(EDGE, bf16)
    to_left, to_right = call(
        k_edges,
        [edge, edge],
        [frames_far, hidden_far, cell_far],
        far=(0, 1, 2),
        scratch=[
            pltpu.VMEM((2, 2, ROWS, 16, CH), bf16),
            pltpu.VMEM((2, ROWS, 16, CH), bf16),
            pltpu.VMEM((2, ROWS, 16, CH), f32),
            pltpu.SemaphoreType.DMA((6,)),
        ],
        part=2.0,
    )
    left, right = both_ways("gx", to_left, to_right)
    w = pltpu.with_memory_space_constraint(conv_weight[0].reshape(9, 512, GATES), pltpu.VMEM)
    (acc_a,) = call(k_hidden, [sums], [hidden_init, w], scratch=[pltpu.VMEM(STACK, bf16)], part=0.4)

    def swap_cores(x):
        return lax.ppermute(x, "layer", swap)

    def hold(x):
        return call(k_nothing, [vm(x.shape, x.dtype)], [x], aliases={0: 0})[0]

    lent = swap_cores(call(k_lend, [row], [hidden_init, left, right])[0])
    acc_a, cx = call(
        k_sides,
        [sums, tile32],
        [hidden_init, cell_init, w, left, right, acc_a],
        aliases={5: 0},
        scratch=[pltpu.VMEM((3, ROWS, 32, CH), bf16)],
        part=0.1,
    )
    two_rows = vm((2, EXT, CH), bf16)
    rows, later = call(k_rows, [two_rows, two_rows], [frames, hidden_init, left, right, lent])
    mine, mine_later = swap_rows(rows), swap_rows(later)
    stack = vm(STACK, bf16)
    acc_a, next_stack = call(
        k_frame,
        [sums, stack],
        [frames, w, left, right, acc_a],
        aliases={4: 0},
        scratch=[pltpu.VMEM(STACK, bf16)],
        part=0.45,
    )
    acc_b, cx, h = call(k_next, [sums, tile32, tile], [next_stack, w, bias, acc_a, cx], aliases={4: 1}, part=0.22)
    mine = hold(mine)
    other = swap_cores(mine)
    (acc_b,) = call(k_rest, [sums], [next_stack, w, acc_b], aliases={2: 0}, part=0.22)
    mine_later = hold(mine_later)
    other_later = swap_cores(mine_later)
    acc_a, h, cx = call(
        k_first,
        [sums, tile, tile32],
        [mine, other, w, bias, cx, h, acc_a],
        aliases={4: 2, 5: 1, 6: 0},
        scratch=[pltpu.VMEM((2,) + PAIR, bf16)],
        part=0.3,
    )

    recv = swap_cores(h)
    acc_a, acc_b = call(
        k_second,
        [sums, sums],
        [mine_later, other_later, w, acc_a, acc_b],
        aliases={3: 0, 4: 1},
        scratch=[pltpu.VMEM(PAIR, bf16)],
        part=0.5,
    )
    mine = swap_rows(call(k_pick, [row], [h, recv])[0])
    acc_a, acc_b, cx, h2, s = call(
        k_third,
        [sums, sums, tile32, tile, stack],
        [h, recv, w, bias, cx, acc_a, acc_b],
        aliases={4: 2, 5: 0, 6: 1},
        part=0.25,
    )
    mine = hold(mine)
    other = swap_cores(mine)
    acc_a, acc_b = call(k_ends, [sums, sums], [w, s, acc_a, acc_b], aliases={2: 0, 3: 1}, part=0.2)
    acc_a, acc_b, cx, h, out = call(
        k_fourth,
        [sums, sums, tile32, tile, row],
        [mine, other, w, bias, cx, h2, acc_a, acc_b],
        aliases={4: 2, 5: 3, 6: 0, 7: 1},
        scratch=[pltpu.VMEM(PAIR, bf16)],
        part=0.2,
    )

    recv = swap_cores(h)
    mine = swap_rows(out)
    acc_b, s = call(k_fifth, [sums, vm(CENTER, bf16)], [h, w, acc_b], aliases={2: 0}, part=0.22)
    mine_lent = swap_rows(call(k_lent, [row], [recv])[0])
    hv, cv = vm((1, ROWS, COLS, CH), bf16), vm((1, ROWS, COLS, CH), f32)
    acc_b, s = call(k_sixth, [sums, vm(CENTER, bf16)], [recv, w, s, acc_b], aliases={3: 0}, part=0.45)
    (mine,) = call(k_join, [two_rows], [mine, mine_lent])
    other = swap_cores(mine)
    acc_b, hid, cell = call(k_seventh, [sums, hv, cv], [h, cx, w, bias, s, acc_b], aliases={5: 0}, part=0.25)
    _, ho, co = call(
        k_last,
        [sums, hv, cv],
        [mine, other, cx, w, bias, hid, cell, acc_b],
        aliases={5: 1, 6: 2, 7: 0},
        scratch=[pltpu.VMEM((2, 3, 2, COLS, CH), bf16)],
        part=0.3,
    )
    return ho, co


def solution(mesh):
    placed = (
        P(None, "gy", "gx", None),
        P("layer", "gy", "gx", None),
        P("layer", "gy", "gx", None),
        P("layer", None, None),
        P(),
    )
    return jax.shard_map(
        per_device,
        mesh=mesh,
        in_specs=placed,
        out_specs=(P("layer", "gy", "gx", None), P("layer", "gy", "gx", None)),
        check_vma=False,
    )
```

```python
import jax
import jax.numpy as jnp
from jax import lax
from jax.experimental import pallas as pl
from jax.experimental.pallas import tpu as pltpu
from jax.sharding import PartitionSpec as P

f32 = jnp.float32
bf16 = jnp.bfloat16
ROWS, COLS, CH, GATES = 4, 256, 256, 1024
PAD = 8
EXT = COLS + 2 * PAD
LO, HI = 16, EXT - 16
NB = 512
UNIT = 2 * ROWS * COLS * 4608 * 1024
ACC = (ROWS, EXT, GATES)
TILE = (ROWS, EXT, CH)
STACK = (3, ROWS, EXT, CH)
PAIR = (3, 2, EXT, CH)
EDGE = (20, PAD, CH)

CENTER = (3, ROWS, COLS, CH)
GROUP = CH // 2

ANYV = pl.BlockSpec(memory_space=pltpu.VMEM)
HBM = pl.BlockSpec(memory_space=pltpu.HBM)


def vm(shape, dtype):
    return pltpu.VMEM(shape, dtype)


class Chain:
    def __init__(self):
        self.mark = ()

    def __call__(self, body, outs, args, aliases=None, scratch=(), part=0.0, limit=8, far=(), far_out=()):
        flat, tree = jax.tree.flatten(list(args))
        places = jax.tree.unflatten(tree, range(len(flat)))
        aliases = {places[i]: o for i, o in (aliases or {}).items()}
        given, marks, made = len(flat), len(self.mark), len(outs)

        def kernel(*refs):
            first = given + marks
            inputs = jax.tree.unflatten(tree, refs[:given])
            return body(*inputs, *refs[first : first + made], *refs[first + made + 1 :])

        *results, mark = pl.pallas_call(
            kernel,
            in_specs=[HBM if i in far else ANYV for i in range(given)] + [ANYV] * marks,
            out_specs=[HBM if i in far_out else ANYV for i in range(made)] + [ANYV],
            out_shape=list(outs) + [vm((8, 128), f32)],
            scratch_shapes=list(scratch),
            input_output_aliases=aliases,
            compiler_params=pltpu.CompilerParams(vmem_limit_bytes=limit << 20),
            cost_estimate=pl.CostEstimate(flops=int(UNIT * part), bytes_accessed=1 << 20, transcendentals=0),
        )(*flat, *self.mark)
        self.mark = (mark,)
        return results


def far(x):
    return pltpu.with_memory_space_constraint(x, pltpu.HBM)


def core_is(k):
    return pl.when(lax.axis_index("layer") == k)


def inside(axis, step):
    at = lax.axis_index(axis) + step
    return jnp.logical_and(at >= 0, at < lax.axis_size(axis)).astype(f32)


def build(stack, r, x):
    x = x.astype(f32)
    stack[0, r] = pltpu.roll(x, 1, 0).astype(bf16)
    stack[1, r] = x.astype(bf16)
    stack[2, r] = pltpu.roll(x, EXT - 1, 0).astype(bf16)


def widen(row, left, right):
    a = left.astype(f32) * inside("gx", -1)
    b = right.astype(f32) * inside("gx", 1)
    return jnp.concatenate([a, row.astype(f32), b], axis=0)


def bare(row):
    zero = jnp.zeros((PAD, CH), f32)
    return jnp.concatenate([zero, row.astype(f32), zero], axis=0)


def build_center(stack, r, x):
    x = x.astype(f32)
    for dx, y in ((0, pltpu.roll(x, 1, 0)), (1, x), (2, pltpu.roll(x, EXT - 1, 0))):
        stack[dx, r] = y[PAD : PAD + COLS].astype(bf16)


BLOCKS = range(GATES // NB)


def block(n):
    return slice(n * NB, (n + 1) * NB) if isinstance(n, int) else pl.ds(pl.multiple_of(n * NB, NB), NB)


def each_block(body):
    def step(n, carry):
        body(n)
        return carry

    lax.fori_loop(0, GATES // NB, step, 0)


def taps(w, n, lhs, off, tap, total):
    d = jnp.dot(lhs, w[tap, off : off + 256, block(n)], preferred_element_type=f32)
    return d if total is None else total + d


def inner(acc, w, stack, off, n, r, lo, hi, add):
    c = block(n)
    total = acc[r, lo:hi, c] if add else None
    for dy in range(3):
        q = r + dy - 1
        if 0 <= q < ROWS:
            for dx in range(3):
                total = taps(w, n, stack[dx, q, lo:hi, :], off, 3 * dy + dx, total)
    acc[r, lo:hi, c] = total


ENDS = ((0, 0, 0), (ROWS - 1, 1, 2))


def outer(acc, w, parts, n, end, m=EXT):
    r, q, dy = ENDS[end]
    c = slice(n * NB, (n + 1) * NB)
    total = acc[r, 0:m, c]
    for dx in range(3):
        for stack, off in parts:
            total = taps(w, n, stack[dx, q], off, 3 * dy + dx, total)
    acc[r, 0:m, c] = total


def sigmoid(x):
    return 0.5 * jnp.tanh(0.5 * x) + 0.5


def gates_at(acc, bias, layer, r, n, at, cell):
    def gate(i):
        b = bias[layer : layer + 1, i * CH + n * GROUP : i * CH + (n + 1) * GROUP]
        return acc[r, at, i * CH + n * GROUP : i * CH + (n + 1) * GROUP] + b

    cell = sigmoid(gate(1)) * cell + sigmoid(gate(0)) * jnp.tanh(gate(3))
    return cell, sigmoid(gate(2)) * jnp.tanh(cell)


def finish(acc, bias, layer, r, n, cx, h):
    ch = slice(n * GROUP, (n + 1) * GROUP)
    for k in range(EXT // 16):
        at = slice(k * 16, (k + 1) * 16)
        new, hid = gates_at(acc, bias, layer, r, n, at, cx[r, at, ch])
        cx[r, at, ch] = new
        if k in (0, EXT // 16 - 1):
            half = lax.broadcasted_iota(jnp.int32, (16, GROUP), 0) < PAD
            kept = half if k else jnp.logical_not(half)
            hid = hid * jnp.where(kept, 1.0, inside("gx", 1 if k else -1))
        h[r, at, ch] = hid.astype(bf16)


def ends(acc, w, parts, bias, layer, cx, h):
    for n in BLOCKS:
        outer(acc, w, parts, n, 0)
    for n in BLOCKS:
        outer(acc, w, parts, n, 1)
        finish(acc, bias, layer, 0, n, cx, h)
    for n in BLOCKS:
        finish(acc, bias, layer, ROWS - 1, n, cx, h)


def finish_center(acc, bias, r, n, cx, hv, cv):
    ch = slice(n * GROUP, (n + 1) * GROUP)
    for k in range(COLS // 16):
        at = slice(k * 16, (k + 1) * 16)
        src = slice(k * 16 + PAD, (k + 1) * 16 + PAD)
        new, hid = gates_at(acc, bias, 1, r, n, at, cx[r, src, ch])
        cv[r, at, ch] = new
        hv[r, at, ch] = hid.astype(bf16)


def k_edges(fr, hid, cell, to_left, to_right, fs, hs, cs, sem):
    jobs = []
    for side, a in ((0, 0), (1, COLS - 16)):
        jobs.append((fr.at[:, :, a : a + 16, :], fs.at[side]))
        jobs.append((hid.at[0, :, a : a + 16, :], hs.at[side]))
        jobs.append((cell.at[0, :, a : a + 16, :], cs.at[side]))
    copies = [pltpu.make_async_copy(src, dst, sem.at[i]) for i, (src, dst) in enumerate(jobs)]
    for c in copies:
        c.start()
    for c in copies:
        c.wait()
    for side, out, at in ((0, to_left, slice(0, PAD)), (1, to_right, slice(PAD, 16))):
        for r in range(ROWS):
            out[r] = fs[side, 0, r, at]
            out[4 + r] = fs[side, 1, r, at]
            out[8 + r] = hs[side, r, at]
            c = cs[side, r, at]
            hi = c.astype(bf16)
            out[12 + r] = hi
            out[16 + r] = (c - hi.astype(f32)).astype(bf16)


def k_hidden(hid, w, acc, s):
    for r in range(ROWS):
        build(s, r, bare(hid[0, r]))

    def body(n):
        for r in range(ROWS):
            inner(acc, w, s, 256, n, r, LO, HI, False)

    each_block(body)


def below():
    return lax.rem(lax.axis_index("layer") + lax.axis_index("gy"), 2) == 0


def my_row():
    return jnp.where(below(), ROWS - 1, 0)


def halo(s, mine, other, make=None):
    make = make or build
    mine, other = mine.astype(f32), other.astype(f32)
    make(s, 0, jnp.where(below(), other, mine) * inside("gy", -1))
    make(s, 1, jnp.where(below(), mine, other) * inside("gy", 1))


def k_lend(hid, left, right, out):
    r = ROWS - 1 - my_row()
    out[...] = widen(hid[0, r], left[8 + r], right[8 + r]).astype(bf16)


def k_rows(fr, hid, left, right, lent, out, later):
    r = my_row()
    own = widen(hid[0, r], left[8 + r], right[8 + r])
    lent = lent[...].astype(f32)
    first = lax.axis_index("layer") == 0
    out[0] = widen(fr[0, r], left[r], right[r]).astype(bf16)
    out[1] = jnp.where(first, own, lent).astype(bf16)
    later[0] = widen(fr[1, r], left[4 + r], right[4 + r]).astype(bf16)
    later[1] = jnp.where(first, lent, own).astype(bf16)


def k_sides(hid, cell, w, left, right, acc_in, acc, cx, t):
    for r in range(ROWS):
        a = left[12 + r].astype(f32) + left[16 + r].astype(f32)
        b = right[12 + r].astype(f32) + right[16 + r].astype(f32)
        cx[r] = jnp.concatenate([a, cell[0, r], b], axis=0)
        x = widen(hid[0, r], left[8 + r], right[8 + r])
        for dx, y in ((0, pltpu.roll(x, 1, 0)), (1, x), (2, pltpu.roll(x, EXT - 1, 0))):
            t[dx, r, 0:16] = y[0:16].astype(bf16)
            t[dx, r, 16:32] = y[HI:EXT].astype(bf16)
    for n in BLOCKS:
        c = slice(n * NB, (n + 1) * NB)
        total = None
        for dy in range(3):
            m = ROWS if dy == 1 else ROWS - 1
            first = max(dy - 1, 0)
            for dx in range(3):
                lhs = t[dx, first : first + m].reshape(m * 32, CH)
                d = taps(w, n, lhs, 256, 3 * dy + dx, None)
                zero = jnp.zeros((32, NB), f32)
                if dy == 0:
                    d = jnp.concatenate([zero, d], axis=0)
                if dy == 2:
                    d = jnp.concatenate([d, zero], axis=0)
                total = d if total is None else total + d
        for r in range(ROWS):
            acc[r, 0:LO, c] = total[r * 32 : r * 32 + 16]
            acc[r, HI:EXT, c] = total[r * 32 + 16 : r * 32 + 32]


def k_frame(fr, w, left, right, acc_in, acc, s1, s):
    @core_is(0)
    def _():
        def frame(dst, i, r):
            build(dst, r, widen(fr[i, r], left[4 * i + r], right[4 * i + r]))

        for r in range(ROWS):
            frame(s, 0, r)

        def body(n):
            for r in range(ROWS):
                inner(acc, w, s, 0, n, r, 0, EXT, True)

        each_block(body)
        for r in range(ROWS):
            frame(s1, 1, r)


def k_next(s1, w, bias, acc_in, cx_in, acc_b, cx, h):
    @core_is(0)
    def _():
        for r in range(ROWS):
            inner(acc_b, w, s1, 0, 0, r, 0, EXT, False)
            finish(acc_in, bias, 0, 1 + r // 2, r % 2, cx, h)


def k_rest(s1, w, b_in, acc_b):
    @core_is(0)
    def _():
        for r in range(ROWS):
            inner(acc_b, w, s1, 0, 1, r, 0, EXT, False)


def k_first(mine, other, w, bias, cx_in, h_in, acc_in, acc, h, cx, s):
    @core_is(0)
    def _():
        halo(s.at[0], mine[0], other[0])
        halo(s.at[1], mine[1], other[1])
        ends(acc, w, ((s.at[0], 0), (s.at[1], 256)), bias, 0, cx, h)


def k_second(mine, other, w, a_in, b_in, acc_a, acc_b, s):
    def work(i, acc, off):
        halo(s, mine[i], other[i])
        for end in (0, 1):
            for n in BLOCKS:
                outer(acc, w, ((s, off),), n, end)

    @core_is(0)
    def _():
        work(0, acc_b, 0)

    @core_is(1)
    def _():
        work(1, acc_a, 256)


def k_pick(h, recv, out):
    r = my_row()

    @core_is(0)
    def _():
        out[...] = h[r]

    @core_is(1)
    def _():
        out[...] = recv[r]


def k_third(h_in, recv, w, bias, cx_in, a_in, b_in, acc_a, acc_b, cx, h, s):
    def work(src, acc, off, layer):
        build(s, 0, src[0])
        build(s, 1, src[1])
        for r in (1, 2):
            build(s, r + 1, src[r + 1])
            for n in BLOCKS:
                inner(acc, w, s, off, n, r, 0, EXT, True)
                if r == 2:
                    finish(acc, bias, layer, 1, n, cx, h)
        for n in BLOCKS:
            finish(acc, bias, layer, 2, n, cx, h)

    @core_is(0)
    def _():
        work(h_in, acc_b, 256, 0)

    @core_is(1)
    def _():
        work(recv, acc_a, 0, 1)


def k_ends(w, s, a_in, b_in, acc_a, acc_b):
    def work(acc, off):
        for n in BLOCKS:
            for r in (0, ROWS - 1):
                inner(acc, w, s, off, n, r, 0, EXT, True)

    @core_is(0)
    def _():
        work(acc_b, 256)

    @core_is(1)
    def _():
        work(acc_a, 0)


def k_nothing(x_in, x):
    pass


def k_fourth(mine, other, w, bias, cx_in, h_in, a_in, b_in, acc_a, acc_b, cx, h, out, s):
    halo(s, mine[...], other[...])

    def work(acc, off, layer):
        ends(acc, w, ((s, off),), bias, layer, cx, h)

    @core_is(0)
    def _():
        work(acc_b, 256, 0)

    @core_is(1)
    def _():
        work(acc_a, 0, 1)

    out[...] = h[my_row()]


def k_fifth(h, w, acc_in, acc, s):
    @core_is(1)
    def _():
        build_center(s, 0, h[0])
        build_center(s, 1, h[1])
        for r in range(ROWS):
            if r + 2 < ROWS:
                build_center(s, r + 2, h[r + 2])
            inner(acc, w, s, 256, 0, r, 0, COLS, False)


def k_lent(recv, out):
    out[...] = recv[my_row()]


def k_join(own, lent, out):
    core = lax.axis_index("layer")
    out[core] = own[...]
    out[1 - core] = lent[...]


def k_sixth(recv, w, s1, acc_in, acc, s):
    @core_is(1)
    def _():
        for r in range(ROWS):
            inner(acc, w, s1, 256, 1, r, 0, COLS, False)
            build_center(s, r, recv[r])
        for r in range(ROWS):
            inner(acc, w, s, 0, 0, r, 0, COLS, True)


def k_seventh(h, cx, w, bias, s, acc_in, acc, hv, cv):
    @core_is(0)
    def _():
        for r in range(ROWS):
            hv[r] = h[r].astype(f32)[PAD : PAD + COLS].astype(bf16)
            cv[r] = cx[r, PAD : PAD + COLS]

    @core_is(1)
    def _():
        for r, done in ((1, None), (2, 1), (0, 2), (3, None)):
            inner(acc, w, s, 0, 1, r, 0, COLS, True)
            if done:
                for n in BLOCKS:
                    finish_center(acc, bias, done, n, cx, hv, cv)


def k_last(mine, other, cx, w, bias, hv_in, cv_in, acc_in, acc, hv, cv, ho, co, s, sem):
    def out(r):
        return (
            pltpu.make_async_copy(hv.at[r], ho.at[0, r], sem.at[0, r]),
            pltpu.make_async_copy(cv.at[r], co.at[0, r], sem.at[1, r]),
        )

    def send(r):
        for c in out(r):
            c.start()

    for r in (1, 2):
        send(r)

    @core_is(1)
    def _():
        halo(s.at[0], mine[0], other[0], build_center)
        halo(s.at[1], mine[1], other[1], build_center)
        for end in (0, 1):
            for n in BLOCKS:
                outer(acc, w, ((s.at[0], 0), (s.at[1], 256)), n, end, COLS)
                if end:
                    finish_center(acc, bias, 0, n, cx, hv, cv)
        send(0)
        for n in BLOCKS:
            finish_center(acc, bias, ROWS - 1, n, cx, hv, cv)
        send(ROWS - 1)

    @core_is(0)
    def _():
        for r in (0, 3):
            send(r)

    for r in range(ROWS):
        for c in out(r):
            c.wait()


def swap_rows(x):
    ny, nx = lax.axis_size("gy"), lax.axis_size("gx")
    pairs = []
    for core in range(2):
        for y in range(ny):
            to = (y + 1 if (core + y) % 2 == 0 else y - 1) % ny
            pairs += [((core * ny + y) * nx + x, (core * ny + to) * nx + x) for x in range(nx)]
    return lax.ppermute(x, ("layer", "gy", "gx"), pairs)


def both_ways(axis, to_low, to_high):
    n = lax.axis_size(axis)
    from_low = lax.ppermute(to_high, axis, [(i, (i + 1) % n) for i in range(n)])
    from_high = lax.ppermute(to_low, axis, [(i, (i - 1) % n) for i in range(n)])
    return from_low, from_high


def per_device(frames, hidden_init, cell_init, conv_weight, conv_bias):
    call = Chain()
    bias = conv_bias
    frames_far, hidden_far, cell_far = far(frames), far(hidden_init), far(cell_init)
    swap = [(0, 1), (1, 0)]
    sums, tile, tile32, row = vm(ACC, f32), vm(TILE, bf16), vm(TILE, f32), vm((EXT, CH), bf16)

    edge = vm(EDGE, bf16)
    to_left, to_right = call(
        k_edges,
        [edge, edge],
        [frames_far, hidden_far, cell_far],
        far=(0, 1, 2),
        scratch=[
            pltpu.VMEM((2, 2, ROWS, 16, CH), bf16),
            pltpu.VMEM((2, ROWS, 16, CH), bf16),
            pltpu.VMEM((2, ROWS, 16, CH), f32),
            pltpu.SemaphoreType.DMA((6,)),
        ],
        part=2.0,
    )
    left, right = both_ways("gx", to_left, to_right)
    w = pltpu.with_memory_space_constraint(conv_weight[0].reshape(9, 512, GATES), pltpu.VMEM)
    (acc_a,) = call(k_hidden, [sums], [hidden_init, w], scratch=[pltpu.VMEM(STACK, bf16)], part=0.4)

    def swap_cores(x):
        return lax.ppermute(x, "layer", swap)

    def hold(x):
        return call(k_nothing, [vm(x.shape, x.dtype)], [x], aliases={0: 0})[0]

    lent = swap_cores(call(k_lend, [row], [hidden_init, left, right])[0])
    acc_a, cx = call(
        k_sides,
        [sums, tile32],
        [hidden_init, cell_init, w, left, right, acc_a],
        aliases={5: 0},
        scratch=[pltpu.VMEM((3, ROWS, 32, CH), bf16)],
        part=0.1,
    )
    two_rows = vm((2, EXT, CH), bf16)
    rows, later = call(k_rows, [two_rows, two_rows], [frames, hidden_init, left, right, lent])
    mine, mine_later = swap_rows(rows), swap_rows(later)
    stack = vm(STACK, bf16)
    acc_a, next_stack = call(
        k_frame,
        [sums, stack],
        [frames, w, left, right, acc_a],
        aliases={4: 0},
        scratch=[pltpu.VMEM(STACK, bf16)],
        part=0.45,
    )
    acc_b, cx, h = call(k_next, [sums, tile32, tile], [next_stack, w, bias, acc_a, cx], aliases={4: 1}, part=0.22)
    mine = hold(mine)
    other = swap_cores(mine)
    (acc_b,) = call(k_rest, [sums], [next_stack, w, acc_b], aliases={2: 0}, part=0.22)
    mine_later = hold(mine_later)
    other_later = swap_cores(mine_later)
    acc_a, h, cx = call(
        k_first,
        [sums, tile, tile32],
        [mine, other, w, bias, cx, h, acc_a],
        aliases={4: 2, 5: 1, 6: 0},
        scratch=[pltpu.VMEM((2,) + PAIR, bf16)],
        part=0.3,
    )

    recv = swap_cores(h)
    acc_a, acc_b = call(
        k_second,
        [sums, sums],
        [mine_later, other_later, w, acc_a, acc_b],
        aliases={3: 0, 4: 1},
        scratch=[pltpu.VMEM(PAIR, bf16)],
        part=0.5,
    )
    mine = swap_rows(call(k_pick, [row], [h, recv])[0])
    acc_a, acc_b, cx, h2, s = call(
        k_third,
        [sums, sums, tile32, tile, stack],
        [h, recv, w, bias, cx, acc_a, acc_b],
        aliases={4: 2, 5: 0, 6: 1},
        part=0.25,
    )
    mine = hold(mine)
    other = swap_cores(mine)
    acc_a, acc_b = call(k_ends, [sums, sums], [w, s, acc_a, acc_b], aliases={2: 0, 3: 1}, part=0.2)
    acc_a, acc_b, cx, h, out = call(
        k_fourth,
        [sums, sums, tile32, tile, row],
        [mine, other, w, bias, cx, h2, acc_a, acc_b],
        aliases={4: 2, 5: 3, 6: 0, 7: 1},
        scratch=[pltpu.VMEM(PAIR, bf16)],
        part=0.2,
    )

    recv = swap_cores(h)
    mine = swap_rows(out)
    acc_b, s = call(k_fifth, [sums, vm(CENTER, bf16)], [h, w, acc_b], aliases={2: 0}, part=0.22)
    mine_lent = swap_rows(call(k_lent, [row], [recv])[0])
    hv, cv = vm((ROWS, COLS, CH), bf16), vm((ROWS, COLS, CH), f32)
    acc_b, s = call(k_sixth, [sums, vm(CENTER, bf16)], [recv, w, s, acc_b], aliases={3: 0}, part=0.45)
    (mine,) = call(k_join, [two_rows], [mine, mine_lent])
    other = swap_cores(mine)
    acc_b, hid, cell = call(k_seventh, [sums, hv, cv], [h, cx, w, bias, s, acc_b], aliases={5: 0}, part=0.25)
    _, _, _, ho, co = call(
        k_last,
        [
            sums,
            hv,
            cv,
            jax.ShapeDtypeStruct((1, ROWS, COLS, CH), bf16),
            jax.ShapeDtypeStruct((1, ROWS, COLS, CH), f32),
        ],
        [mine, other, cx, w, bias, hid, cell, acc_b],
        aliases={5: 1, 6: 2, 7: 0},
        far_out=(3, 4),
        scratch=[pltpu.VMEM((2, 3, 2, COLS, CH), bf16), pltpu.SemaphoreType.DMA((2, ROWS))],
        part=0.3,
    )
    return ho, co


def solution(mesh):
    placed = (
        P(None, "gy", "gx", None),
        P("layer", "gy", "gx", None),
        P("layer", "gy", "gx", None),
        P("layer", None, None),
        P(),
    )
    return jax.shard_map(
        per_device,
        mesh=mesh,
        in_specs=placed,
        out_specs=(P("layer", "gy", "gx", None), P("layer", "gy", "gx", None)),
        check_vma=False,
    )
```

```python
import jax
import jax.numpy as jnp
from jax import lax
from jax.experimental import pallas as pl
from jax.experimental.pallas import tpu as pltpu
from jax.sharding import PartitionSpec as P

f32 = jnp.float32
bf16 = jnp.bfloat16
ROWS, COLS, CH, GATES = 4, 256, 256, 1024
PAD = 8
EXT = COLS + 2 * PAD
LO, HI = 16, EXT - 16
NB = 512
UNIT = 2 * ROWS * COLS * 4608 * 1024
ACC = (ROWS, EXT, GATES)
TILE = (ROWS, EXT, CH)
STACK = (3, ROWS, EXT, CH)
PAIR = (3, 2, EXT, CH)
EDGE = (20, PAD, CH)

CENTER = (3, ROWS, COLS, CH)
GROUP = CH // 2

ANYV = pl.BlockSpec(memory_space=pltpu.VMEM)
HBM = pl.BlockSpec(memory_space=pltpu.HBM)


def vm(shape, dtype):
    return pltpu.VMEM(shape, dtype)


class Chain:
    def __init__(self):
        self.mark = ()

    def __call__(self, body, outs, args, aliases=None, scratch=(), part=0.0, limit=8, far=(), far_out=()):
        flat, tree = jax.tree.flatten(list(args))
        places = jax.tree.unflatten(tree, range(len(flat)))
        aliases = {places[i]: o for i, o in (aliases or {}).items()}
        given, marks, made = len(flat), len(self.mark), len(outs)

        def kernel(*refs):
            first = given + marks
            inputs = jax.tree.unflatten(tree, refs[:given])
            return body(*inputs, *refs[first : first + made], *refs[first + made + 1 :])

        *results, mark = pl.pallas_call(
            kernel,
            in_specs=[HBM if i in far else ANYV for i in range(given)] + [ANYV] * marks,
            out_specs=[HBM if i in far_out else ANYV for i in range(made)] + [ANYV],
            out_shape=list(outs) + [vm((8, 128), f32)],
            scratch_shapes=list(scratch),
            input_output_aliases=aliases,
            compiler_params=pltpu.CompilerParams(vmem_limit_bytes=limit << 20),
            cost_estimate=pl.CostEstimate(flops=int(UNIT * part), bytes_accessed=1 << 20, transcendentals=0),
        )(*flat, *self.mark)
        self.mark = (mark,)
        return results


def far(x):
    return pltpu.with_memory_space_constraint(x, pltpu.HBM)


def core_is(k):
    return pl.when(lax.axis_index("layer") == k)


def inside(axis, step):
    at = lax.axis_index(axis) + step
    return jnp.logical_and(at >= 0, at < lax.axis_size(axis)).astype(f32)


def build(stack, r, x):
    x = x.astype(f32)
    stack[0, r] = pltpu.roll(x, 1, 0).astype(bf16)
    stack[1, r] = x.astype(bf16)
    stack[2, r] = pltpu.roll(x, EXT - 1, 0).astype(bf16)


def widen(row, left, right):
    a = left.astype(f32) * inside("gx", -1)
    b = right.astype(f32) * inside("gx", 1)
    return jnp.concatenate([a, row.astype(f32), b], axis=0)


def bare(row):
    zero = jnp.zeros((PAD, CH), f32)
    return jnp.concatenate([zero, row.astype(f32), zero], axis=0)


def build_center(stack, r, x):
    x = x.astype(f32)
    for dx, y in ((0, pltpu.roll(x, 1, 0)), (1, x), (2, pltpu.roll(x, EXT - 1, 0))):
        stack[dx, r] = y[PAD : PAD + COLS].astype(bf16)


BLOCKS = range(GATES // NB)


def block(n):
    return slice(n * NB, (n + 1) * NB) if isinstance(n, int) else pl.ds(pl.multiple_of(n * NB, NB), NB)


def each_block(body):
    def step(n, carry):
        body(n)
        return carry

    lax.fori_loop(0, GATES // NB, step, 0)


def taps(w, n, lhs, off, tap, total):
    d = jnp.dot(lhs, w[tap, off : off + 256, block(n)], preferred_element_type=f32)
    return d if total is None else total + d


def inner(acc, w, stack, off, n, r, lo, hi, add):
    c = block(n)
    total = acc[r, lo:hi, c] if add else None
    for dy in range(3):
        q = r + dy - 1
        if 0 <= q < ROWS:
            for dx in range(3):
                total = taps(w, n, stack[dx, q, lo:hi, :], off, 3 * dy + dx, total)
    acc[r, lo:hi, c] = total


ENDS = ((0, 0, 0), (ROWS - 1, 1, 2))


def outer(acc, w, parts, n, end, m=EXT):
    r, q, dy = ENDS[end]
    c = slice(n * NB, (n + 1) * NB)
    total = acc[r, 0:m, c]
    for dx in range(3):
        for stack, off in parts:
            total = taps(w, n, stack[dx, q], off, 3 * dy + dx, total)
    acc[r, 0:m, c] = total


def sigmoid(x):
    return 0.5 * jnp.tanh(0.5 * x) + 0.5


def gates_at(acc, bias, layer, r, n, at, cell):
    def gate(i):
        b = bias[layer : layer + 1, i * CH + n * GROUP : i * CH + (n + 1) * GROUP]
        return acc[r, at, i * CH + n * GROUP : i * CH + (n + 1) * GROUP] + b

    cell = sigmoid(gate(1)) * cell + sigmoid(gate(0)) * jnp.tanh(gate(3))
    return cell, sigmoid(gate(2)) * jnp.tanh(cell)


def finish(acc, bias, layer, r, n, cx, h):
    ch = slice(n * GROUP, (n + 1) * GROUP)
    for k in range(EXT // 16):
        at = slice(k * 16, (k + 1) * 16)
        new, hid = gates_at(acc, bias, layer, r, n, at, cx[r, at, ch])
        cx[r, at, ch] = new
        if k in (0, EXT // 16 - 1):
            half = lax.broadcasted_iota(jnp.int32, (16, GROUP), 0) < PAD
            kept = half if k else jnp.logical_not(half)
            hid = hid * jnp.where(kept, 1.0, inside("gx", 1 if k else -1))
        h[r, at, ch] = hid.astype(bf16)


def ends(acc, w, parts, bias, layer, cx, h):
    for n in BLOCKS:
        outer(acc, w, parts, n, 0)
    for n in BLOCKS:
        outer(acc, w, parts, n, 1)
        finish(acc, bias, layer, 0, n, cx, h)
    for n in BLOCKS:
        finish(acc, bias, layer, ROWS - 1, n, cx, h)


def finish_center(acc, bias, r, n, cx, hv, cv):
    ch = slice(n * GROUP, (n + 1) * GROUP)
    for k in range(COLS // 16):
        at = slice(k * 16, (k + 1) * 16)
        src = slice(k * 16 + PAD, (k + 1) * 16 + PAD)
        new, hid = gates_at(acc, bias, 1, r, n, at, cx[r, src, ch])
        cv[r, at, ch] = new
        hv[r, at, ch] = hid.astype(bf16)


def k_edges(fr, hid, cell, to_left, to_right, fs, hs, cs, sem):
    jobs = []
    for side, a in ((0, 0), (1, COLS - 16)):
        jobs.append((fr.at[:, :, a : a + 16, :], fs.at[side]))
        jobs.append((hid.at[0, :, a : a + 16, :], hs.at[side]))
        jobs.append((cell.at[0, :, a : a + 16, :], cs.at[side]))
    copies = [pltpu.make_async_copy(src, dst, sem.at[i]) for i, (src, dst) in enumerate(jobs)]
    for c in copies:
        c.start()
    for c in copies:
        c.wait()
    for side, out, at in ((0, to_left, slice(0, PAD)), (1, to_right, slice(PAD, 16))):
        for r in range(ROWS):
            out[r] = fs[side, 0, r, at]
            out[4 + r] = fs[side, 1, r, at]
            out[8 + r] = hs[side, r, at]
            c = cs[side, r, at]
            hi = c.astype(bf16)
            out[12 + r] = hi
            out[16 + r] = (c - hi.astype(f32)).astype(bf16)


def k_hidden(hid, w, acc, s):
    for r in range(ROWS):
        build(s, r, bare(hid[0, r]))

    def body(n):
        for r in range(ROWS):
            inner(acc, w, s, 256, n, r, LO, HI, False)

    each_block(body)


def below(flip=0):
    return lax.rem(lax.axis_index("layer") + lax.axis_index("gy") + flip, 2) == 0


def my_row(flip=0):
    return jnp.where(below(flip), ROWS - 1, 0)


def halo(s, mine, other, make=None, flip=0):
    make = make or build
    mine, other = mine.astype(f32), other.astype(f32)
    make(s, 0, jnp.where(below(flip), other, mine) * inside("gy", -1))
    make(s, 1, jnp.where(below(flip), mine, other) * inside("gy", 1))


def k_lend(hid, left, right, out):
    r = ROWS - 1 - my_row()
    out[...] = widen(hid[0, r], left[8 + r], right[8 + r]).astype(bf16)


def k_rows(fr, hid, left, right, lent, out, later):
    r = my_row()
    own = widen(hid[0, r], left[8 + r], right[8 + r])
    lent = lent[...].astype(f32)
    first = lax.axis_index("layer") == 0
    out[0] = widen(fr[0, r], left[r], right[r]).astype(bf16)
    out[1] = jnp.where(first, own, lent).astype(bf16)
    later[0] = widen(fr[1, r], left[4 + r], right[4 + r]).astype(bf16)
    later[1] = jnp.where(first, lent, own).astype(bf16)


def k_sides(hid, cell, w, left, right, acc_in, acc, cx, t):
    for r in range(ROWS):
        a = left[12 + r].astype(f32) + left[16 + r].astype(f32)
        b = right[12 + r].astype(f32) + right[16 + r].astype(f32)
        cx[r] = jnp.concatenate([a, cell[0, r], b], axis=0)
        x = widen(hid[0, r], left[8 + r], right[8 + r])
        for dx, y in ((0, pltpu.roll(x, 1, 0)), (1, x), (2, pltpu.roll(x, EXT - 1, 0))):
            t[dx, r, 0:16] = y[0:16].astype(bf16)
            t[dx, r, 16:32] = y[HI:EXT].astype(bf16)
    for n in BLOCKS:
        c = slice(n * NB, (n + 1) * NB)
        total = None
        for dy in range(3):
            m = ROWS if dy == 1 else ROWS - 1
            first = max(dy - 1, 0)
            for dx in range(3):
                lhs = t[dx, first : first + m].reshape(m * 32, CH)
                d = taps(w, n, lhs, 256, 3 * dy + dx, None)
                zero = jnp.zeros((32, NB), f32)
                if dy == 0:
                    d = jnp.concatenate([zero, d], axis=0)
                if dy == 2:
                    d = jnp.concatenate([d, zero], axis=0)
                total = d if total is None else total + d
        for r in range(ROWS):
            acc[r, 0:LO, c] = total[r * 32 : r * 32 + 16]
            acc[r, HI:EXT, c] = total[r * 32 + 16 : r * 32 + 32]


def k_frame(fr, w, left, right, acc_in, acc, s1, s):
    @core_is(0)
    def _():
        def frame(dst, i, r):
            build(dst, r, widen(fr[i, r], left[4 * i + r], right[4 * i + r]))

        for r in range(ROWS):
            frame(s, 0, r)

        def body(n):
            for r in range(ROWS):
                inner(acc, w, s, 0, n, r, 0, EXT, True)

        each_block(body)
        for r in range(ROWS):
            frame(s1, 1, r)


def k_next(s1, w, bias, acc_in, cx_in, acc_b, cx, h):
    @core_is(0)
    def _():
        for r in range(ROWS):
            inner(acc_b, w, s1, 0, 0, r, 0, EXT, False)
            finish(acc_in, bias, 0, 1 + r // 2, r % 2, cx, h)


def k_rest(s1, w, b_in, acc_b):
    @core_is(0)
    def _():
        for r in range(ROWS):
            inner(acc_b, w, s1, 0, 1, r, 0, EXT, False)


def k_first(mine, other, w, bias, cx_in, h_in, acc_in, acc, h, cx, s):
    @core_is(0)
    def _():
        halo(s.at[0], mine[0], other[0])
        halo(s.at[1], mine[1], other[1])
        ends(acc, w, ((s.at[0], 0), (s.at[1], 256)), bias, 0, cx, h)


def k_second(mine, other, w, a_in, b_in, acc_a, acc_b, s):
    def work(i, acc, off):
        halo(s, mine[i], other[i])
        for end in (0, 1):
            for n in BLOCKS:
                outer(acc, w, ((s, off),), n, end)

    @core_is(0)
    def _():
        work(0, acc_b, 0)

    @core_is(1)
    def _():
        work(1, acc_a, 256)


def k_pick(h, recv, out):
    r = my_row()

    @core_is(0)
    def _():
        out[...] = h[r]

    @core_is(1)
    def _():
        out[...] = recv[r]


def k_third(h_in, recv, w, bias, cx_in, a_in, b_in, acc_a, acc_b, cx, h, s):
    def work(src, acc, off, layer):
        build(s, 0, src[0])
        build(s, 1, src[1])
        for r in (1, 2):
            build(s, r + 1, src[r + 1])
            for n in BLOCKS:
                inner(acc, w, s, off, n, r, 0, EXT, True)
                if r == 2:
                    finish(acc, bias, layer, 1, n, cx, h)
        for n in BLOCKS:
            finish(acc, bias, layer, 2, n, cx, h)

    @core_is(0)
    def _():
        work(h_in, acc_b, 256, 0)

    @core_is(1)
    def _():
        work(recv, acc_a, 0, 1)


def k_ends(w, s, a_in, b_in, acc_a, acc_b):
    def work(acc, off):
        for n in BLOCKS:
            for r in (0, ROWS - 1):
                inner(acc, w, s, off, n, r, 0, EXT, True)

    @core_is(0)
    def _():
        work(acc_b, 256)

    @core_is(1)
    def _():
        work(acc_a, 0)


def k_nothing(x_in, x):
    pass


def k_fourth(mine, other, w, bias, cx_in, h_in, a_in, b_in, acc_a, acc_b, cx, h, out, s):
    halo(s, mine[...], other[...])

    def work(acc, off, layer):
        ends(acc, w, ((s, off),), bias, layer, cx, h)

    @core_is(0)
    def _():
        work(acc_b, 256, 0)

    @core_is(1)
    def _():
        work(acc_a, 0, 1)

    out[...] = h[my_row(1)]


def k_fifth(h, w, acc_in, acc, s):
    @core_is(1)
    def _():
        build_center(s, 0, h[0])
        build_center(s, 1, h[1])
        for r in range(ROWS):
            if r + 2 < ROWS:
                build_center(s, r + 2, h[r + 2])
            inner(acc, w, s, 256, 0, r, 0, COLS, False)


def k_lent(recv, out):
    out[...] = recv[my_row(1)]


def k_join(own, lent, out):
    core = lax.axis_index("layer")
    out[core] = own[...]
    out[1 - core] = lent[...]


def k_sixth(recv, w, s1, acc_in, acc, s):
    @core_is(1)
    def _():
        for r in range(ROWS):
            inner(acc, w, s1, 256, 1, r, 0, COLS, False)
            build_center(s, r, recv[r])
        for r in range(ROWS):
            inner(acc, w, s, 0, 0, r, 0, COLS, True)


def k_seventh(h, cx, w, bias, s, acc_in, acc, hv, cv):
    @core_is(0)
    def _():
        for r in range(ROWS):
            hv[r] = h[r].astype(f32)[PAD : PAD + COLS].astype(bf16)
            cv[r] = cx[r, PAD : PAD + COLS]

    @core_is(1)
    def _():
        for r, done in ((1, None), (2, 1), (0, 2), (3, None)):
            inner(acc, w, s, 0, 1, r, 0, COLS, True)
            if done:
                for n in BLOCKS:
                    finish_center(acc, bias, done, n, cx, hv, cv)


def k_last(mine, other, cx, w, bias, hv_in, cv_in, acc_in, acc, hv, cv, ho, co, s, sem):
    def out(r):
        return (
            pltpu.make_async_copy(hv.at[r], ho.at[0, r], sem.at[0, r]),
            pltpu.make_async_copy(cv.at[r], co.at[0, r], sem.at[1, r]),
        )

    def send(r):
        for c in out(r):
            c.start()

    for r in (1, 2):
        send(r)

    @core_is(1)
    def _():
        halo(s.at[0], mine[0], other[0], build_center, 1)
        halo(s.at[1], mine[1], other[1], build_center, 1)
        for end in (0, 1):
            for n in BLOCKS:
                outer(acc, w, ((s.at[0], 0), (s.at[1], 256)), n, end, COLS)
                if end:
                    finish_center(acc, bias, 0, n, cx, hv, cv)
        send(0)
        for n in BLOCKS:
            finish_center(acc, bias, ROWS - 1, n, cx, hv, cv)
        send(ROWS - 1)

    @core_is(0)
    def _():
        for r in (0, 3):
            send(r)

    for r in range(ROWS):
        for c in out(r):
            c.wait()


def swap_rows(x, flip=0):
    ny, nx = lax.axis_size("gy"), lax.axis_size("gx")
    pairs = []
    for core in range(2):
        for y in range(ny):
            to = (y + 1 if (core + y + flip) % 2 == 0 else y - 1) % ny
            pairs += [((core * ny + y) * nx + x, (core * ny + to) * nx + x) for x in range(nx)]
    return lax.ppermute(x, ("layer", "gy", "gx"), pairs)


def both_ways(axis, to_low, to_high):
    n = lax.axis_size(axis)
    from_low = lax.ppermute(to_high, axis, [(i, (i + 1) % n) for i in range(n)])
    from_high = lax.ppermute(to_low, axis, [(i, (i - 1) % n) for i in range(n)])
    return from_low, from_high


def per_device(frames, hidden_init, cell_init, conv_weight, conv_bias):
    call = Chain()
    bias = conv_bias
    frames_far, hidden_far, cell_far = far(frames), far(hidden_init), far(cell_init)
    swap = [(0, 1), (1, 0)]
    sums, tile, tile32, row = vm(ACC, f32), vm(TILE, bf16), vm(TILE, f32), vm((EXT, CH), bf16)

    edge = vm(EDGE, bf16)
    to_left, to_right = call(
        k_edges,
        [edge, edge],
        [frames_far, hidden_far, cell_far],
        far=(0, 1, 2),
        scratch=[
            pltpu.VMEM((2, 2, ROWS, 16, CH), bf16),
            pltpu.VMEM((2, ROWS, 16, CH), bf16),
            pltpu.VMEM((2, ROWS, 16, CH), f32),
            pltpu.SemaphoreType.DMA((6,)),
        ],
        part=2.0,
    )
    left, right = both_ways("gx", to_left, to_right)
    w = pltpu.with_memory_space_constraint(conv_weight[0].reshape(9, 512, GATES), pltpu.VMEM)
    (acc_a,) = call(k_hidden, [sums], [hidden_init, w], scratch=[pltpu.VMEM(STACK, bf16)], part=0.4)

    def swap_cores(x):
        return lax.ppermute(x, "layer", swap)

    def hold(x):
        return call(k_nothing, [vm(x.shape, x.dtype)], [x], aliases={0: 0})[0]

    lent = swap_cores(call(k_lend, [row], [hidden_init, left, right])[0])
    acc_a, cx = call(
        k_sides,
        [sums, tile32],
        [hidden_init, cell_init, w, left, right, acc_a],
        aliases={5: 0},
        scratch=[pltpu.VMEM((3, ROWS, 32, CH), bf16)],
        part=0.1,
    )
    two_rows = vm((2, EXT, CH), bf16)
    rows, later = call(k_rows, [two_rows, two_rows], [frames, hidden_init, left, right, lent])
    mine, mine_later = swap_rows(rows), swap_rows(later)
    stack = vm(STACK, bf16)
    acc_a, next_stack = call(
        k_frame,
        [sums, stack],
        [frames, w, left, right, acc_a],
        aliases={4: 0},
        scratch=[pltpu.VMEM(STACK, bf16)],
        part=0.45,
    )
    acc_b, cx, h = call(k_next, [sums, tile32, tile], [next_stack, w, bias, acc_a, cx], aliases={4: 1}, part=0.22)
    mine = hold(mine)
    other = swap_cores(mine)
    (acc_b,) = call(k_rest, [sums], [next_stack, w, acc_b], aliases={2: 0}, part=0.22)
    mine_later = hold(mine_later)
    other_later = swap_cores(mine_later)
    acc_a, h, cx = call(
        k_first,
        [sums, tile, tile32],
        [mine, other, w, bias, cx, h, acc_a],
        aliases={4: 2, 5: 1, 6: 0},
        scratch=[pltpu.VMEM((2,) + PAIR, bf16)],
        part=0.3,
    )

    recv = swap_cores(h)
    acc_a, acc_b = call(
        k_second,
        [sums, sums],
        [mine_later, other_later, w, acc_a, acc_b],
        aliases={3: 0, 4: 1},
        scratch=[pltpu.VMEM(PAIR, bf16)],
        part=0.5,
    )
    mine = swap_rows(call(k_pick, [row], [h, recv])[0])
    acc_a, acc_b, cx, h2, s = call(
        k_third,
        [sums, sums, tile32, tile, stack],
        [h, recv, w, bias, cx, acc_a, acc_b],
        aliases={4: 2, 5: 0, 6: 1},
        part=0.25,
    )
    mine = hold(mine)
    other = swap_cores(mine)
    acc_a, acc_b = call(k_ends, [sums, sums], [w, s, acc_a, acc_b], aliases={2: 0, 3: 1}, part=0.2)
    acc_a, acc_b, cx, h, out = call(
        k_fourth,
        [sums, sums, tile32, tile, row],
        [mine, other, w, bias, cx, h2, acc_a, acc_b],
        aliases={4: 2, 5: 3, 6: 0, 7: 1},
        scratch=[pltpu.VMEM(PAIR, bf16)],
        part=0.2,
    )

    recv = swap_cores(h)
    mine = swap_rows(out, 1)
    acc_b, s = call(k_fifth, [sums, vm(CENTER, bf16)], [h, w, acc_b], aliases={2: 0}, part=0.22)
    mine_lent = swap_rows(call(k_lent, [row], [recv])[0], 1)
    hv, cv = vm((ROWS, COLS, CH), bf16), vm((ROWS, COLS, CH), f32)
    acc_b, s = call(k_sixth, [sums, vm(CENTER, bf16)], [recv, w, s, acc_b], aliases={3: 0}, part=0.45)
    (mine,) = call(k_join, [two_rows], [mine, mine_lent])
    other = swap_cores(mine)
    acc_b, hid, cell = call(k_seventh, [sums, hv, cv], [h, cx, w, bias, s, acc_b], aliases={5: 0}, part=0.25)
    _, _, _, ho, co = call(
        k_last,
        [
            sums,
            hv,
            cv,
            jax.ShapeDtypeStruct((1, ROWS, COLS, CH), bf16),
            jax.ShapeDtypeStruct((1, ROWS, COLS, CH), f32),
        ],
        [mine, other, cx, w, bias, hid, cell, acc_b],
        aliases={5: 1, 6: 2, 7: 0},
        far_out=(3, 4),
        scratch=[pltpu.VMEM((2, 3, 2, COLS, CH), bf16), pltpu.SemaphoreType.DMA((2, ROWS))],
        part=0.3,
    )
    return ho, co


def solution(mesh):
    placed = (
        P(None, "gy", "gx", None),
        P("layer", "gy", "gx", None),
        P("layer", "gy", "gx", None),
        P("layer", None, None),
        P(),
    )
    return jax.shard_map(
        per_device,
        mesh=mesh,
        in_specs=placed,
        out_specs=(P("layer", "gy", "gx", None), P("layer", "gy", "gx", None)),
        check_vma=False,
    )
```

```python
import jax
import jax.numpy as jnp
from jax import lax
from jax.experimental import pallas as pl
from jax.experimental.pallas import tpu as pltpu
from jax.sharding import PartitionSpec as P

f32 = jnp.float32
bf16 = jnp.bfloat16
ROWS, COLS, CH, GATES = 4, 256, 256, 1024
PAD = 8
EXT = COLS + 2 * PAD
LO, HI = 16, EXT - 16
NB = 512
UNIT = 2 * ROWS * COLS * 4608 * 1024
ACC = (ROWS, EXT, GATES)
TILE = (ROWS, EXT, CH)
STACK = (3, ROWS, EXT, CH)
PAIR = (3, 2, EXT, CH)
EDGE = (20, PAD, CH)

CENTER = (3, ROWS, COLS, CH)
GROUP = CH // 2

ANYV = pl.BlockSpec(memory_space=pltpu.VMEM)
HBM = pl.BlockSpec(memory_space=pltpu.HBM)


def vm(shape, dtype):
    return pltpu.VMEM(shape, dtype)


class Chain:
    def __init__(self):
        self.mark = ()

    def __call__(self, body, outs, args, aliases=None, scratch=(), part=0.0, limit=8, far=(), far_out=()):
        flat, tree = jax.tree.flatten(list(args))
        places = jax.tree.unflatten(tree, range(len(flat)))
        aliases = {places[i]: o for i, o in (aliases or {}).items()}
        given, marks, made = len(flat), len(self.mark), len(outs)

        def kernel(*refs):
            first = given + marks
            inputs = jax.tree.unflatten(tree, refs[:given])
            return body(*inputs, *refs[first : first + made], *refs[first + made + 1 :])

        *results, mark = pl.pallas_call(
            kernel,
            in_specs=[HBM if i in far else ANYV for i in range(given)] + [ANYV] * marks,
            out_specs=[HBM if i in far_out else ANYV for i in range(made)] + [ANYV],
            out_shape=list(outs) + [vm((8, 128), f32)],
            scratch_shapes=list(scratch),
            input_output_aliases=aliases,
            compiler_params=pltpu.CompilerParams(vmem_limit_bytes=limit << 20),
            cost_estimate=pl.CostEstimate(flops=int(UNIT * part), bytes_accessed=1 << 20, transcendentals=0),
        )(*flat, *self.mark)
        self.mark = (mark,)
        return results


def far(x):
    return pltpu.with_memory_space_constraint(x, pltpu.HBM)


def core_is(k):
    return pl.when(lax.axis_index("layer") == k)


def inside(axis, step):
    at = lax.axis_index(axis) + step
    return jnp.logical_and(at >= 0, at < lax.axis_size(axis)).astype(f32)


def build(stack, r, x):
    x = x.astype(f32)
    stack[0, r] = pltpu.roll(x, 1, 0).astype(bf16)
    stack[1, r] = x.astype(bf16)
    stack[2, r] = pltpu.roll(x, EXT - 1, 0).astype(bf16)


def widen(row, left, right):
    a = left.astype(f32) * inside("gx", -1)
    b = right.astype(f32) * inside("gx", 1)
    return jnp.concatenate([a, row.astype(f32), b], axis=0)


def bare(row):
    zero = jnp.zeros((PAD, CH), f32)
    return jnp.concatenate([zero, row.astype(f32), zero], axis=0)


def build_center(stack, r, x):
    x = x.astype(f32)
    for dx, y in ((0, pltpu.roll(x, 1, 0)), (1, x), (2, pltpu.roll(x, EXT - 1, 0))):
        stack[dx, r] = y[PAD : PAD + COLS].astype(bf16)


BLOCKS = range(GATES // NB)


def block(n):
    return slice(n * NB, (n + 1) * NB) if isinstance(n, int) else pl.ds(pl.multiple_of(n * NB, NB), NB)


def each_block(body):
    def step(n, carry):
        body(n)
        return carry

    lax.fori_loop(0, GATES // NB, step, 0)


def taps(w, n, lhs, off, tap, total):
    d = jnp.dot(lhs, w[tap, off : off + 256, block(n)], preferred_element_type=f32)
    return d if total is None else total + d


def inner(acc, w, stack, off, n, r, lo, hi, add):
    c = block(n)
    total = acc[r, lo:hi, c] if add else None
    for dy in range(3):
        q = r + dy - 1
        if 0 <= q < ROWS:
            for dx in range(3):
                total = taps(w, n, stack[dx, q, lo:hi, :], off, 3 * dy + dx, total)
    acc[r, lo:hi, c] = total


ENDS = ((0, 0, 0), (ROWS - 1, 1, 2))


def outer(acc, w, parts, n, end, m=EXT):
    r, q, dy = ENDS[end]
    c = slice(n * NB, (n + 1) * NB)
    total = acc[r, 0:m, c]
    for dx in range(3):
        for stack, off in parts:
            total = taps(w, n, stack[dx, q], off, 3 * dy + dx, total)
    acc[r, 0:m, c] = total


def sigmoid(x):
    return 0.5 * jnp.tanh(0.5 * x) + 0.5


def gates_at(acc, bias, layer, r, n, at, cell):
    def gate(i):
        b = bias[layer : layer + 1, i * CH + n * GROUP : i * CH + (n + 1) * GROUP]
        return acc[r, at, i * CH + n * GROUP : i * CH + (n + 1) * GROUP] + b

    cell = sigmoid(gate(1)) * cell + sigmoid(gate(0)) * jnp.tanh(gate(3))
    return cell, sigmoid(gate(2)) * jnp.tanh(cell)


def finish(acc, bias, layer, r, n, cx, h):
    ch = slice(n * GROUP, (n + 1) * GROUP)
    for k in range(EXT // 16):
        at = slice(k * 16, (k + 1) * 16)
        new, hid = gates_at(acc, bias, layer, r, n, at, cx[r, at, ch])
        cx[r, at, ch] = new
        if k in (0, EXT // 16 - 1):
            half = lax.broadcasted_iota(jnp.int32, (16, GROUP), 0) < PAD
            kept = half if k else jnp.logical_not(half)
            hid = hid * jnp.where(kept, 1.0, inside("gx", 1 if k else -1))
        h[r, at, ch] = hid.astype(bf16)


def ends(acc, w, parts, bias, layer, cx, h):
    for n in BLOCKS:
        outer(acc, w, parts, n, 0)
    for n in BLOCKS:
        outer(acc, w, parts, n, 1)
        finish(acc, bias, layer, 0, n, cx, h)
    for n in BLOCKS:
        finish(acc, bias, layer, ROWS - 1, n, cx, h)


def finish_center(acc, bias, r, n, cx, hv, cv):
    ch = slice(n * GROUP, (n + 1) * GROUP)
    for k in range(COLS // 16):
        at = slice(k * 16, (k + 1) * 16)
        src = slice(k * 16 + PAD, (k + 1) * 16 + PAD)
        new, hid = gates_at(acc, bias, 1, r, n, at, cx[r, src, ch])
        cv[r, at, ch] = new
        hv[r, at, ch] = hid.astype(bf16)


def k_edges(fr, hid, cell, to_left, to_right, fs, hs, cs, sem):
    jobs = []
    for side, a in ((0, 0), (1, COLS - 16)):
        jobs.append((fr.at[:, :, a : a + 16, :], fs.at[side]))
        jobs.append((hid.at[0, :, a : a + 16, :], hs.at[side]))
        jobs.append((cell.at[0, :, a : a + 16, :], cs.at[side]))
    copies = [pltpu.make_async_copy(src, dst, sem.at[i]) for i, (src, dst) in enumerate(jobs)]
    for c in copies:
        c.start()
    for c in copies:
        c.wait()
    for side, out, at in ((0, to_left, slice(0, PAD)), (1, to_right, slice(PAD, 16))):
        for r in range(ROWS):
            out[r] = fs[side, 0, r, at]
            out[4 + r] = fs[side, 1, r, at]
            out[8 + r] = hs[side, r, at]
            c = cs[side, r, at]
            hi = c.astype(bf16)
            out[12 + r] = hi
            out[16 + r] = (c - hi.astype(f32)).astype(bf16)


def k_hidden(hid, w, acc, s):
    for r in range(ROWS):
        build(s, r, bare(hid[0, r]))

    def body(n):
        for r in range(ROWS):
            inner(acc, w, s, 256, n, r, LO, HI, False)

    each_block(body)


def below(flip=0):
    return lax.rem(lax.axis_index("layer") + lax.axis_index("gy") + flip, 2) == 0


def my_row(flip=0):
    return jnp.where(below(flip), ROWS - 1, 0)


def halo(s, mine, other, make=None, flip=0):
    make = make or build
    mine, other = mine.astype(f32), other.astype(f32)
    make(s, 0, jnp.where(below(flip), other, mine) * inside("gy", -1))
    make(s, 1, jnp.where(below(flip), mine, other) * inside("gy", 1))


def k_lend(hid, left, right, out):
    r = ROWS - 1 - my_row()
    out[...] = widen(hid[0, r], left[8 + r], right[8 + r]).astype(bf16)


def k_rows(fr, hid, left, right, lent, out, later):
    r = my_row()
    own = widen(hid[0, r], left[8 + r], right[8 + r])
    lent = lent[...].astype(f32)
    first = lax.axis_index("layer") == 0
    out[0] = widen(fr[0, r], left[r], right[r]).astype(bf16)
    out[1] = jnp.where(first, own, lent).astype(bf16)
    later[0] = widen(fr[1, r], left[4 + r], right[4 + r]).astype(bf16)
    later[1] = jnp.where(first, lent, own).astype(bf16)


def k_sides(hid, cell, w, left, right, acc_in, acc, cx, t):
    for r in range(ROWS):
        a = left[12 + r].astype(f32) + left[16 + r].astype(f32)
        b = right[12 + r].astype(f32) + right[16 + r].astype(f32)
        cx[r] = jnp.concatenate([a, cell[0, r], b], axis=0)
        x = widen(hid[0, r], left[8 + r], right[8 + r])
        for dx, y in ((0, pltpu.roll(x, 1, 0)), (1, x), (2, pltpu.roll(x, EXT - 1, 0))):
            t[dx, r, 0:16] = y[0:16].astype(bf16)
            t[dx, r, 16:32] = y[HI:EXT].astype(bf16)
    for n in BLOCKS:
        c = slice(n * NB, (n + 1) * NB)
        total = None
        for dy in range(3):
            m = ROWS if dy == 1 else ROWS - 1
            first = max(dy - 1, 0)
            for dx in range(3):
                lhs = t[dx, first : first + m].reshape(m * 32, CH)
                d = taps(w, n, lhs, 256, 3 * dy + dx, None)
                zero = jnp.zeros((32, NB), f32)
                if dy == 0:
                    d = jnp.concatenate([zero, d], axis=0)
                if dy == 2:
                    d = jnp.concatenate([d, zero], axis=0)
                total = d if total is None else total + d
        for r in range(ROWS):
            acc[r, 0:LO, c] = total[r * 32 : r * 32 + 16]
            acc[r, HI:EXT, c] = total[r * 32 + 16 : r * 32 + 32]


def k_frame(fr, w, left, right, acc_in, acc, s1, s):
    @core_is(0)
    def _():
        def frame(dst, i, r):
            build(dst, r, widen(fr[i, r], left[4 * i + r], right[4 * i + r]))

        for r in range(ROWS):
            frame(s, 0, r)

        def body(n):
            for r in range(ROWS):
                inner(acc, w, s, 0, n, r, 0, EXT, True)

        each_block(body)
        for r in range(ROWS):
            frame(s1, 1, r)


def k_next(s1, w, bias, acc_in, cx_in, acc_b, cx, h):
    @core_is(0)
    def _():
        for r in range(ROWS):
            inner(acc_b, w, s1, 0, 0, r, 0, EXT, False)
            finish(acc_in, bias, 0, 1 + r // 2, r % 2, cx, h)


def k_rest(s1, w, b_in, acc_b):
    @core_is(0)
    def _():
        for r in range(ROWS):
            inner(acc_b, w, s1, 0, 1, r, 0, EXT, False)


def k_first(mine, other, w, bias, cx_in, h_in, acc_in, acc, h, cx, s):
    @core_is(0)
    def _():
        halo(s.at[0], mine[0], other[0])
        halo(s.at[1], mine[1], other[1])
        ends(acc, w, ((s.at[0], 0), (s.at[1], 256)), bias, 0, cx, h)


def k_second(mine, other, w, a_in, b_in, acc_a, acc_b, s):
    def work(i, acc, off):
        halo(s, mine[i], other[i])
        for end in (0, 1):
            for n in BLOCKS:
                outer(acc, w, ((s, off),), n, end)

    @core_is(0)
    def _():
        work(0, acc_b, 0)

    @core_is(1)
    def _():
        work(1, acc_a, 256)


def k_pick(h, recv, out):
    r = my_row()

    @core_is(0)
    def _():
        out[...] = h[r]

    @core_is(1)
    def _():
        out[...] = recv[r]


def k_third(h_in, recv, w, bias, cx_in, a_in, b_in, acc_a, acc_b, cx, h, s):
    def work(src, acc, off, layer):
        build(s, 0, src[0])
        build(s, 1, src[1])
        for r in (1, 2):
            build(s, r + 1, src[r + 1])
            for n in BLOCKS:
                inner(acc, w, s, off, n, r, 0, EXT, True)
                if r == 2:
                    finish(acc, bias, layer, 1, n, cx, h)
        for n in BLOCKS:
            finish(acc, bias, layer, 2, n, cx, h)

    @core_is(0)
    def _():
        work(h_in, acc_b, 256, 0)

    @core_is(1)
    def _():
        work(recv, acc_a, 0, 1)


def k_ends(w, s, a_in, b_in, acc_a, acc_b):
    def work(acc, off):
        for n in BLOCKS:
            for r in (0, ROWS - 1):
                inner(acc, w, s, off, n, r, 0, EXT, True)

    @core_is(0)
    def _():
        work(acc_b, 256)

    @core_is(1)
    def _():
        work(acc_a, 0)


def k_nothing(x_in, x):
    pass


def k_fourth(mine, other, w, bias, cx_in, h_in, a_in, b_in, acc_a, acc_b, cx, h, s):
    halo(s, mine[...], other[...])

    def work(acc, off, layer):
        ends(acc, w, ((s, off),), bias, layer, cx, h)

    @core_is(0)
    def _():
        work(acc_b, 256, 0)

    @core_is(1)
    def _():
        work(acc_a, 0, 1)


def k_fifth(h, w, acc_in, acc, s):
    @core_is(1)
    def _():
        build_center(s, 0, h[0])
        build_center(s, 1, h[1])
        for r in range(ROWS):
            if r + 2 < ROWS:
                build_center(s, r + 2, h[r + 2])
            inner(acc, w, s, 256, 0, r, 0, COLS, False)


def k_pick_two(h, recv, out):
    r = my_row(1)
    core = lax.axis_index("layer")
    out[core] = h[r]
    out[1 - core] = recv[r]


def k_sixth(recv, w, s1, acc_in, acc, s):
    @core_is(1)
    def _():
        for r in range(ROWS):
            inner(acc, w, s1, 256, 1, r, 0, COLS, False)
            build_center(s, r, recv[r])
        for r in range(ROWS):
            inner(acc, w, s, 0, 0, r, 0, COLS, True)


def k_seventh(h, cx, w, bias, s, acc_in, acc, hv, cv):
    @core_is(0)
    def _():
        for r in range(ROWS):
            hv[r] = h[r].astype(f32)[PAD : PAD + COLS].astype(bf16)
            cv[r] = cx[r, PAD : PAD + COLS]

    @core_is(1)
    def _():
        for r, done in ((1, None), (2, 1), (0, 2), (3, None)):
            inner(acc, w, s, 0, 1, r, 0, COLS, True)
            if done:
                for n in BLOCKS:
                    finish_center(acc, bias, done, n, cx, hv, cv)


def last_row(rows, low, acc, w, bias, cx, hv, cv, s):
    r = jnp.where(low, ROWS - 1, 0)
    first = jnp.where(low, 6, 0)
    real = jnp.where(low, inside("gy", 1), inside("gy", -1))
    for i in range(2):
        x = rows[i].astype(f32) * real
        for dx, y in ((0, pltpu.roll(x, 1, 0)), (1, x), (2, pltpu.roll(x, EXT - 1, 0))):
            s[i, dx] = y[PAD : PAD + COLS].astype(bf16)
    for n in BLOCKS:
        total = acc[r, 0:COLS, block(n)]
        for dx in range(3):
            for i in range(2):
                total = taps(w, n, s[i, dx], 256 * i, first + dx, total)
        acc[r, 0:COLS, block(n)] = total
    for n in BLOCKS:
        finish_center(acc, bias, r, n, cx, hv, cv)


def k_mine(mine, cx, w, bias, hv_in, cv_in, acc_in, acc, hv, cv, s):
    @core_is(1)
    def _():
        last_row(mine, below(1), acc, w, bias, cx, hv, cv, s)


def k_last(other, cx, w, bias, hv_in, cv_in, acc_in, acc, hv, cv, ho, co, s, sem):
    rows = (1, 2, my_row(1), ROWS - 1 - my_row(1))

    def out(k):
        r = rows[k]
        return (
            pltpu.make_async_copy(hv.at[r], ho.at[0, r], sem.at[0, k]),
            pltpu.make_async_copy(cv.at[r], co.at[0, r], sem.at[1, k]),
        )

    for k in range(3):
        for c in out(k):
            c.start()

    @core_is(1)
    def _():
        last_row(other, jnp.logical_not(below(1)), acc, w, bias, cx, hv, cv, s)

    for c in out(3):
        c.start()
    for k in range(ROWS):
        for c in out(k):
            c.wait()


def swap_rows(x, flip=0):
    ny, nx = lax.axis_size("gy"), lax.axis_size("gx")
    pairs = []
    for core in range(2):
        for y in range(ny):
            to = (y + 1 if (core + y + flip) % 2 == 0 else y - 1) % ny
            pairs += [((core * ny + y) * nx + x, (core * ny + to) * nx + x) for x in range(nx)]
    return lax.ppermute(x, ("layer", "gy", "gx"), pairs)


def both_ways(axis, to_low, to_high):
    n = lax.axis_size(axis)
    from_low = lax.ppermute(to_high, axis, [(i, (i + 1) % n) for i in range(n)])
    from_high = lax.ppermute(to_low, axis, [(i, (i - 1) % n) for i in range(n)])
    return from_low, from_high


def per_device(frames, hidden_init, cell_init, conv_weight, conv_bias):
    call = Chain()
    bias = conv_bias
    frames_far, hidden_far, cell_far = far(frames), far(hidden_init), far(cell_init)
    swap = [(0, 1), (1, 0)]
    sums, tile, tile32, row = vm(ACC, f32), vm(TILE, bf16), vm(TILE, f32), vm((EXT, CH), bf16)

    edge = vm(EDGE, bf16)
    to_left, to_right = call(
        k_edges,
        [edge, edge],
        [frames_far, hidden_far, cell_far],
        far=(0, 1, 2),
        scratch=[
            pltpu.VMEM((2, 2, ROWS, 16, CH), bf16),
            pltpu.VMEM((2, ROWS, 16, CH), bf16),
            pltpu.VMEM((2, ROWS, 16, CH), f32),
            pltpu.SemaphoreType.DMA((6,)),
        ],
        part=2.0,
    )
    left, right = both_ways("gx", to_left, to_right)
    w = pltpu.with_memory_space_constraint(conv_weight[0].reshape(9, 512, GATES), pltpu.VMEM)
    (acc_a,) = call(k_hidden, [sums], [hidden_init, w], scratch=[pltpu.VMEM(STACK, bf16)], part=0.4)

    def swap_cores(x):
        return lax.ppermute(x, "layer", swap)

    def hold(x):
        return call(k_nothing, [vm(x.shape, x.dtype)], [x], aliases={0: 0})[0]

    lent = swap_cores(call(k_lend, [row], [hidden_init, left, right])[0])
    acc_a, cx = call(
        k_sides,
        [sums, tile32],
        [hidden_init, cell_init, w, left, right, acc_a],
        aliases={5: 0},
        scratch=[pltpu.VMEM((3, ROWS, 32, CH), bf16)],
        part=0.1,
    )
    two_rows = vm((2, EXT, CH), bf16)
    rows, later = call(k_rows, [two_rows, two_rows], [frames, hidden_init, left, right, lent])
    mine, mine_later = swap_rows(rows), swap_rows(later)
    stack = vm(STACK, bf16)
    acc_a, next_stack = call(
        k_frame,
        [sums, stack],
        [frames, w, left, right, acc_a],
        aliases={4: 0},
        scratch=[pltpu.VMEM(STACK, bf16)],
        part=0.45,
    )
    acc_b, cx, h = call(k_next, [sums, tile32, tile], [next_stack, w, bias, acc_a, cx], aliases={4: 1}, part=0.22)
    mine = hold(mine)
    other = swap_cores(mine)
    (acc_b,) = call(k_rest, [sums], [next_stack, w, acc_b], aliases={2: 0}, part=0.22)
    mine_later = hold(mine_later)
    other_later = swap_cores(mine_later)
    acc_a, h, cx = call(
        k_first,
        [sums, tile, tile32],
        [mine, other, w, bias, cx, h, acc_a],
        aliases={4: 2, 5: 1, 6: 0},
        scratch=[pltpu.VMEM((2,) + PAIR, bf16)],
        part=0.3,
    )

    recv = swap_cores(h)
    acc_a, acc_b = call(
        k_second,
        [sums, sums],
        [mine_later, other_later, w, acc_a, acc_b],
        aliases={3: 0, 4: 1},
        scratch=[pltpu.VMEM(PAIR, bf16)],
        part=0.5,
    )
    mine = swap_rows(call(k_pick, [row], [h, recv])[0])
    acc_a, acc_b, cx, h2, s = call(
        k_third,
        [sums, sums, tile32, tile, stack],
        [h, recv, w, bias, cx, acc_a, acc_b],
        aliases={4: 2, 5: 0, 6: 1},
        part=0.25,
    )
    mine = hold(mine)
    other = swap_cores(mine)
    acc_a, acc_b = call(k_ends, [sums, sums], [w, s, acc_a, acc_b], aliases={2: 0, 3: 1}, part=0.2)
    acc_a, acc_b, cx, h = call(
        k_fourth,
        [sums, sums, tile32, tile],
        [mine, other, w, bias, cx, h2, acc_a, acc_b],
        aliases={4: 2, 5: 3, 6: 0, 7: 1},
        scratch=[pltpu.VMEM(PAIR, bf16)],
        part=0.2,
    )

    recv = swap_cores(h)
    acc_b, s = call(k_fifth, [sums, vm(CENTER, bf16)], [h, w, acc_b], aliases={2: 0}, part=0.22)
    mine = swap_rows(call(k_pick_two, [two_rows], [h, recv])[0], 1)
    hv, cv = vm((ROWS, COLS, CH), bf16), vm((ROWS, COLS, CH), f32)
    acc_b, s = call(k_sixth, [sums, vm(CENTER, bf16)], [recv, w, s, acc_b], aliases={3: 0}, part=0.45)
    acc_b, hid, cell = call(k_seventh, [sums, hv, cv], [h, cx, w, bias, s, acc_b], aliases={5: 0}, part=0.25)
    mine = hold(mine)
    other = swap_cores(mine)
    side = pltpu.VMEM((2, 3, COLS, CH), bf16)
    acc_b, hid, cell = call(
        k_mine,
        [sums, hv, cv],
        [mine, cx, w, bias, hid, cell, acc_b],
        aliases={4: 1, 5: 2, 6: 0},
        scratch=[side],
        part=0.2,
    )
    _, _, _, ho, co = call(
        k_last,
        [
            sums,
            hv,
            cv,
            jax.ShapeDtypeStruct((1, ROWS, COLS, CH), bf16),
            jax.ShapeDtypeStruct((1, ROWS, COLS, CH), f32),
        ],
        [other, cx, w, bias, hid, cell, acc_b],
        aliases={4: 1, 5: 2, 6: 0},
        far_out=(3, 4),
        scratch=[side, pltpu.SemaphoreType.DMA((2, ROWS))],
        part=0.2,
    )
    return ho, co


def solution(mesh):
    placed = (
        P(None, "gy", "gx", None),
        P("layer", "gy", "gx", None),
        P("layer", "gy", "gx", None),
        P("layer", None, None),
        P(),
    )
    return jax.shard_map(
        per_device,
        mesh=mesh,
        in_specs=placed,
        out_specs=(P("layer", "gy", "gx", None), P("layer", "gy", "gx", None)),
        check_vma=False,
    )
```

```python
import jax
import jax.numpy as jnp
from jax import lax
from jax.experimental import pallas as pl
from jax.experimental.pallas import tpu as pltpu
from jax.sharding import PartitionSpec as P

f32 = jnp.float32
bf16 = jnp.bfloat16
ROWS, COLS, CH, GATES = 4, 256, 256, 1024
PAD = 8
EXT = COLS + 2 * PAD
LO, HI = 16, EXT - 16
NB = 512
UNIT = 2 * ROWS * COLS * 4608 * 1024
ACC = (ROWS, EXT, GATES)
TILE = (ROWS, EXT, CH)
STACK = (3, ROWS, EXT, CH)
PAIR = (3, 2, EXT, CH)
EDGE = (20, PAD, CH)

CENTER = (3, ROWS, COLS, CH)
GROUP = CH // 2

ANYV = pl.BlockSpec(memory_space=pltpu.VMEM)
HBM = pl.BlockSpec(memory_space=pltpu.HBM)


def vm(shape, dtype):
    return pltpu.VMEM(shape, dtype)


class Chain:
    def __init__(self):
        self.mark = ()

    def __call__(self, body, outs, args, aliases=None, scratch=(), part=0.0, limit=8, far=(), far_out=()):
        flat, tree = jax.tree.flatten(list(args))
        places = jax.tree.unflatten(tree, range(len(flat)))
        aliases = {places[i]: o for i, o in (aliases or {}).items()}
        given, marks, made = len(flat), len(self.mark), len(outs)

        def kernel(*refs):
            first = given + marks
            inputs = jax.tree.unflatten(tree, refs[:given])
            return body(*inputs, *refs[first : first + made], *refs[first + made + 1 :])

        *results, mark = pl.pallas_call(
            kernel,
            in_specs=[HBM if i in far else ANYV for i in range(given)] + [ANYV] * marks,
            out_specs=[HBM if i in far_out else ANYV for i in range(made)] + [ANYV],
            out_shape=list(outs) + [vm((8, 128), f32)],
            scratch_shapes=list(scratch),
            input_output_aliases=aliases,
            compiler_params=pltpu.CompilerParams(vmem_limit_bytes=limit << 20),
            cost_estimate=pl.CostEstimate(flops=int(UNIT * part), bytes_accessed=1 << 20, transcendentals=0),
        )(*flat, *self.mark)
        self.mark = (mark,)
        return results


def far(x):
    return pltpu.with_memory_space_constraint(x, pltpu.HBM)


def core_is(k):
    return pl.when(lax.axis_index("layer") == k)


def inside(axis, step):
    at = lax.axis_index(axis) + step
    return jnp.logical_and(at >= 0, at < lax.axis_size(axis)).astype(f32)


def build(stack, r, x):
    x = x.astype(f32)
    stack[0, r] = pltpu.roll(x, 1, 0).astype(bf16)
    stack[1, r] = x.astype(bf16)
    stack[2, r] = pltpu.roll(x, EXT - 1, 0).astype(bf16)


def widen(row, left, right):
    a = left.astype(f32) * inside("gx", -1)
    b = right.astype(f32) * inside("gx", 1)
    return jnp.concatenate([a, row.astype(f32), b], axis=0)


def bare(row):
    zero = jnp.zeros((PAD, CH), f32)
    return jnp.concatenate([zero, row.astype(f32), zero], axis=0)


def build_center(stack, r, x):
    x = x.astype(f32)
    for dx, y in ((0, pltpu.roll(x, 1, 0)), (1, x), (2, pltpu.roll(x, EXT - 1, 0))):
        stack[dx, r] = y[PAD : PAD + COLS].astype(bf16)


BLOCKS = range(GATES // NB)


def block(n):
    return slice(n * NB, (n + 1) * NB) if isinstance(n, int) else pl.ds(pl.multiple_of(n * NB, NB), NB)


def each_block(body):
    def step(n, carry):
        body(n)
        return carry

    lax.fori_loop(0, GATES // NB, step, 0)


def taps(w, n, lhs, off, tap, total):
    d = jnp.dot(lhs, w[tap, off : off + 256, block(n)], preferred_element_type=f32)
    return d if total is None else total + d


def inner(acc, w, stack, off, n, r, lo, hi, add):
    c = block(n)
    total = acc[r, lo:hi, c] if add else None
    for dy in range(3):
        q = r + dy - 1
        if 0 <= q < ROWS:
            for dx in range(3):
                total = taps(w, n, stack[dx, q, lo:hi, :], off, 3 * dy + dx, total)
    acc[r, lo:hi, c] = total


ENDS = ((0, 0, 0), (ROWS - 1, 1, 2))


def outer(acc, w, parts, n, end, m=EXT):
    r, q, dy = ENDS[end]
    c = slice(n * NB, (n + 1) * NB)
    total = acc[r, 0:m, c]
    for dx in range(3):
        for stack, off in parts:
            total = taps(w, n, stack[dx, q], off, 3 * dy + dx, total)
    acc[r, 0:m, c] = total


def sigmoid(x):
    return 0.5 * jnp.tanh(0.5 * x) + 0.5


def gates_at(acc, bias, layer, r, n, at, cell):
    def gate(i):
        b = bias[layer : layer + 1, i * CH + n * GROUP : i * CH + (n + 1) * GROUP]
        return acc[r, at, i * CH + n * GROUP : i * CH + (n + 1) * GROUP] + b

    cell = sigmoid(gate(1)) * cell + sigmoid(gate(0)) * jnp.tanh(gate(3))
    return cell, sigmoid(gate(2)) * jnp.tanh(cell)


def finish(acc, bias, layer, r, n, cx, h):
    ch = slice(n * GROUP, (n + 1) * GROUP)
    for k in range(EXT // 16):
        at = slice(k * 16, (k + 1) * 16)
        new, hid = gates_at(acc, bias, layer, r, n, at, cx[r, at, ch])
        cx[r, at, ch] = new
        if k in (0, EXT // 16 - 1):
            half = lax.broadcasted_iota(jnp.int32, (16, GROUP), 0) < PAD
            kept = half if k else jnp.logical_not(half)
            hid = hid * jnp.where(kept, 1.0, inside("gx", 1 if k else -1))
        h[r, at, ch] = hid.astype(bf16)


def ends(acc, w, parts, bias, layer, cx, h):
    for n in BLOCKS:
        outer(acc, w, parts, n, 0)
    for n in BLOCKS:
        outer(acc, w, parts, n, 1)
        finish(acc, bias, layer, 0, n, cx, h)
    for n in BLOCKS:
        finish(acc, bias, layer, ROWS - 1, n, cx, h)


def finish_center(acc, bias, r, n, cx, hv, cv):
    ch = slice(n * GROUP, (n + 1) * GROUP)
    for k in range(COLS // 16):
        at = slice(k * 16, (k + 1) * 16)
        src = slice(k * 16 + PAD, (k + 1) * 16 + PAD)
        new, hid = gates_at(acc, bias, 1, r, n, at, cx[r, src, ch])
        cv[r, at, ch] = new
        hv[r, at, ch] = hid.astype(bf16)


def k_edges(fr, hid, cell, to_left, to_right, fs, hs, cs, sem):
    jobs = []
    for side, a in ((0, 0), (1, COLS - 16)):
        jobs.append((fr.at[:, :, a : a + 16, :], fs.at[side]))
        jobs.append((hid.at[0, :, a : a + 16, :], hs.at[side]))
        jobs.append((cell.at[0, :, a : a + 16, :], cs.at[side]))
    copies = [pltpu.make_async_copy(src, dst, sem.at[i]) for i, (src, dst) in enumerate(jobs)]
    for c in copies:
        c.start()
    for c in copies:
        c.wait()
    for side, out, at in ((0, to_left, slice(0, PAD)), (1, to_right, slice(PAD, 16))):
        for r in range(ROWS):
            out[r] = fs[side, 0, r, at]
            out[4 + r] = fs[side, 1, r, at]
            out[8 + r] = hs[side, r, at]
            c = cs[side, r, at]
            hi = c.astype(bf16)
            out[12 + r] = hi
            out[16 + r] = (c - hi.astype(f32)).astype(bf16)


def k_hidden(hid, w, acc, s):
    for r in range(ROWS):
        build(s, r, bare(hid[0, r]))

    def body(n):
        for r in range(ROWS):
            inner(acc, w, s, 256, n, r, LO, HI, False)

    for n in BLOCKS:
        body(n)


def below(flip=0):
    return lax.rem(lax.axis_index("layer") + lax.axis_index("gy") + flip, 2) == 0


def my_row(flip=0):
    return jnp.where(below(flip), ROWS - 1, 0)


def halo(s, mine, other, make=None, flip=0):
    make = make or build
    mine, other = mine.astype(f32), other.astype(f32)
    make(s, 0, jnp.where(below(flip), other, mine) * inside("gy", -1))
    make(s, 1, jnp.where(below(flip), mine, other) * inside("gy", 1))


def k_lend(hid, left, right, out):
    r = ROWS - 1 - my_row()
    out[...] = widen(hid[0, r], left[8 + r], right[8 + r]).astype(bf16)


def k_rows(fr, hid, left, right, lent, out, later):
    r = my_row()
    own = widen(hid[0, r], left[8 + r], right[8 + r])
    lent = lent[...].astype(f32)
    first = lax.axis_index("layer") == 0
    out[0] = widen(fr[0, r], left[r], right[r]).astype(bf16)
    out[1] = jnp.where(first, own, lent).astype(bf16)
    later[0] = widen(fr[1, r], left[4 + r], right[4 + r]).astype(bf16)
    later[1] = jnp.where(first, lent, own).astype(bf16)


def k_sides(hid, cell, w, left, right, acc_in, acc, cx, t):
    for r in range(ROWS):
        a = left[12 + r].astype(f32) + left[16 + r].astype(f32)
        b = right[12 + r].astype(f32) + right[16 + r].astype(f32)
        cx[r] = jnp.concatenate([a, cell[0, r], b], axis=0)
        x = widen(hid[0, r], left[8 + r], right[8 + r])
        for dx, y in ((0, pltpu.roll(x, 1, 0)), (1, x), (2, pltpu.roll(x, EXT - 1, 0))):
            t[dx, r, 0:16] = y[0:16].astype(bf16)
            t[dx, r, 16:32] = y[HI:EXT].astype(bf16)
    for n in BLOCKS:
        c = slice(n * NB, (n + 1) * NB)
        total = None
        for dy in range(3):
            m = ROWS if dy == 1 else ROWS - 1
            first = max(dy - 1, 0)
            for dx in range(3):
                lhs = t[dx, first : first + m].reshape(m * 32, CH)
                d = taps(w, n, lhs, 256, 3 * dy + dx, None)
                zero = jnp.zeros((32, NB), f32)
                if dy == 0:
                    d = jnp.concatenate([zero, d], axis=0)
                if dy == 2:
                    d = jnp.concatenate([d, zero], axis=0)
                total = d if total is None else total + d
        for r in range(ROWS):
            acc[r, 0:LO, c] = total[r * 32 : r * 32 + 16]
            acc[r, HI:EXT, c] = total[r * 32 + 16 : r * 32 + 32]


def k_frame(fr, w, left, right, acc_in, acc, s1, s):
    @core_is(0)
    def _():
        def frame(dst, i, r):
            build(dst, r, widen(fr[i, r], left[4 * i + r], right[4 * i + r]))

        for r in range(ROWS):
            frame(s, 0, r)

        def body(n):
            for r in range(ROWS):
                inner(acc, w, s, 0, n, r, 0, EXT, True)

        each_block(body)
        for r in range(ROWS):
            frame(s1, 1, r)


def k_next(s1, w, bias, acc_in, cx_in, acc_b, cx, h):
    @core_is(0)
    def _():
        for r in range(ROWS):
            inner(acc_b, w, s1, 0, 0, r, 0, EXT, False)
            finish(acc_in, bias, 0, 1 + r // 2, r % 2, cx, h)


def k_rest(s1, w, b_in, acc_b):
    @core_is(0)
    def _():
        for r in range(ROWS):
            inner(acc_b, w, s1, 0, 1, r, 0, EXT, False)


def k_first(mine, other, w, bias, cx_in, h_in, acc_in, acc, h, cx, s):
    @core_is(0)
    def _():
        halo(s.at[0], mine[0], other[0])
        halo(s.at[1], mine[1], other[1])
        ends(acc, w, ((s.at[0], 0), (s.at[1], 256)), bias, 0, cx, h)


def k_second(mine, other, w, a_in, b_in, acc_a, acc_b, s):
    def work(i, acc, off):
        halo(s, mine[i], other[i])
        for end in (0, 1):
            for n in BLOCKS:
                outer(acc, w, ((s, off),), n, end)

    @core_is(0)
    def _():
        work(0, acc_b, 0)

    @core_is(1)
    def _():
        work(1, acc_a, 256)


def k_pick(h, recv, out):
    r = my_row()

    @core_is(0)
    def _():
        out[...] = h[r]

    @core_is(1)
    def _():
        out[...] = recv[r]


def k_third(h_in, recv, w, bias, cx_in, a_in, b_in, acc_a, acc_b, cx, h, s):
    def work(src, acc, off, layer):
        build(s, 0, src[0])
        build(s, 1, src[1])
        for r in (1, 2):
            build(s, r + 1, src[r + 1])
            for n in BLOCKS:
                inner(acc, w, s, off, n, r, 0, EXT, True)
                if r == 2:
                    finish(acc, bias, layer, 1, n, cx, h)
        for n in BLOCKS:
            finish(acc, bias, layer, 2, n, cx, h)

    @core_is(0)
    def _():
        work(h_in, acc_b, 256, 0)

    @core_is(1)
    def _():
        work(recv, acc_a, 0, 1)


def k_ends(w, s, a_in, b_in, acc_a, acc_b):
    def work(acc, off):
        for n in BLOCKS:
            for r in (0, ROWS - 1):
                inner(acc, w, s, off, n, r, 0, EXT, True)

    @core_is(0)
    def _():
        work(acc_b, 256)

    @core_is(1)
    def _():
        work(acc_a, 0)


def k_nothing(x_in, x):
    pass


def k_fourth(mine, other, w, bias, cx_in, h_in, a_in, b_in, acc_a, acc_b, cx, h, s):
    halo(s, mine[...], other[...])

    def work(acc, off, layer):
        ends(acc, w, ((s, off),), bias, layer, cx, h)

    @core_is(0)
    def _():
        work(acc_b, 256, 0)

    @core_is(1)
    def _():
        work(acc_a, 0, 1)


def k_fifth(h, w, acc_in, acc, s):
    @core_is(1)
    def _():
        build_center(s, 0, h[0])
        build_center(s, 1, h[1])
        for r in range(ROWS):
            if r + 2 < ROWS:
                build_center(s, r + 2, h[r + 2])
            inner(acc, w, s, 256, 0, r, 0, COLS, False)


def k_pick_two(h, recv, out):
    r = my_row(1)
    core = lax.axis_index("layer")
    out[core] = h[r]
    out[1 - core] = recv[r]


def k_sixth(recv, w, s1, acc_in, acc, s):
    @core_is(1)
    def _():
        for r in range(ROWS):
            inner(acc, w, s1, 256, 1, r, 0, COLS, False)
            build_center(s, r, recv[r])
        for r in range(ROWS):
            inner(acc, w, s, 0, 0, r, 0, COLS, True)


def k_seventh(h, cx, w, bias, s, acc_in, acc, hv, cv):
    @core_is(0)
    def _():
        for r in range(ROWS):
            hv[r] = h[r].astype(f32)[PAD : PAD + COLS].astype(bf16)
            cv[r] = cx[r, PAD : PAD + COLS]

    @core_is(1)
    def _():
        for r, done in ((1, None), (2, 1), (0, 2), (3, None)):
            inner(acc, w, s, 0, 1, r, 0, COLS, True)
            if done:
                for n in BLOCKS:
                    finish_center(acc, bias, done, n, cx, hv, cv)


def last_row(rows, low, acc, w, bias, cx, hv, cv, s):
    r = jnp.where(low, ROWS - 1, 0)
    first = jnp.where(low, 6, 0)
    real = jnp.where(low, inside("gy", 1), inside("gy", -1))
    for i in range(2):
        x = rows[i].astype(f32) * real
        for dx, y in ((0, pltpu.roll(x, 1, 0)), (1, x), (2, pltpu.roll(x, EXT - 1, 0))):
            s[i, dx] = y[PAD : PAD + COLS].astype(bf16)
    for n in BLOCKS:
        total = acc[r, 0:COLS, block(n)]
        for dx in range(3):
            for i in range(2):
                total = taps(w, n, s[i, dx], 256 * i, first + dx, total)
        acc[r, 0:COLS, block(n)] = total
    for n in BLOCKS:
        finish_center(acc, bias, r, n, cx, hv, cv)


def k_mine(mine, cx, w, bias, hv_in, cv_in, acc_in, acc, hv, cv, s):
    @core_is(1)
    def _():
        last_row(mine, below(1), acc, w, bias, cx, hv, cv, s)


def k_last(other, cx, w, bias, hv_in, cv_in, acc_in, acc, hv, cv, ho, co, s, sem):
    rows = (1, 2, my_row(1), ROWS - 1 - my_row(1))

    def out(k):
        r = rows[k]
        return (
            pltpu.make_async_copy(hv.at[r], ho.at[0, r], sem.at[0, k]),
            pltpu.make_async_copy(cv.at[r], co.at[0, r], sem.at[1, k]),
        )

    for k in range(3):
        for c in out(k):
            c.start()

    @core_is(1)
    def _():
        last_row(other, jnp.logical_not(below(1)), acc, w, bias, cx, hv, cv, s)

    for c in out(3):
        c.start()
    for k in range(ROWS):
        for c in out(k):
            c.wait()


def swap_rows(x, flip=0):
    ny, nx = lax.axis_size("gy"), lax.axis_size("gx")
    pairs = []
    for core in range(2):
        for y in range(ny):
            to = (y + 1 if (core + y + flip) % 2 == 0 else y - 1) % ny
            pairs += [((core * ny + y) * nx + x, (core * ny + to) * nx + x) for x in range(nx)]
    return lax.ppermute(x, ("layer", "gy", "gx"), pairs)


def both_ways(axis, to_low, to_high):
    n = lax.axis_size(axis)
    from_low = lax.ppermute(to_high, axis, [(i, (i + 1) % n) for i in range(n)])
    from_high = lax.ppermute(to_low, axis, [(i, (i - 1) % n) for i in range(n)])
    return from_low, from_high


def per_device(frames, hidden_init, cell_init, conv_weight, conv_bias):
    call = Chain()
    bias = conv_bias
    frames_far, hidden_far, cell_far = far(frames), far(hidden_init), far(cell_init)
    swap = [(0, 1), (1, 0)]
    sums, tile, tile32, row = vm(ACC, f32), vm(TILE, bf16), vm(TILE, f32), vm((EXT, CH), bf16)

    edge = vm(EDGE, bf16)
    to_left, to_right = call(
        k_edges,
        [edge, edge],
        [frames_far, hidden_far, cell_far],
        far=(0, 1, 2),
        scratch=[
            pltpu.VMEM((2, 2, ROWS, 16, CH), bf16),
            pltpu.VMEM((2, ROWS, 16, CH), bf16),
            pltpu.VMEM((2, ROWS, 16, CH), f32),
            pltpu.SemaphoreType.DMA((6,)),
        ],
        part=2.0,
    )
    left, right = both_ways("gx", to_left, to_right)
    w = pltpu.with_memory_space_constraint(conv_weight[0].reshape(9, 512, GATES), pltpu.VMEM)
    (acc_a,) = call(k_hidden, [sums], [hidden_init, w], scratch=[pltpu.VMEM(STACK, bf16)], part=0.4)

    def swap_cores(x):
        return lax.ppermute(x, "layer", swap)

    def hold(x):
        return call(k_nothing, [vm(x.shape, x.dtype)], [x], aliases={0: 0})[0]

    lent = swap_cores(call(k_lend, [row], [hidden_init, left, right])[0])
    acc_a, cx = call(
        k_sides,
        [sums, tile32],
        [hidden_init, cell_init, w, left, right, acc_a],
        aliases={5: 0},
        scratch=[pltpu.VMEM((3, ROWS, 32, CH), bf16)],
        part=0.1,
    )
    two_rows = vm((2, EXT, CH), bf16)
    rows, later = call(k_rows, [two_rows, two_rows], [frames, hidden_init, left, right, lent])
    mine, mine_later = swap_rows(rows), swap_rows(later)
    stack = vm(STACK, bf16)
    acc_a, next_stack = call(
        k_frame,
        [sums, stack],
        [frames, w, left, right, acc_a],
        aliases={4: 0},
        scratch=[pltpu.VMEM(STACK, bf16)],
        part=0.45,
    )
    acc_b, cx, h = call(k_next, [sums, tile32, tile], [next_stack, w, bias, acc_a, cx], aliases={4: 1}, part=0.22)
    mine = hold(mine)
    other = swap_cores(mine)
    (acc_b,) = call(k_rest, [sums], [next_stack, w, acc_b], aliases={2: 0}, part=0.22)
    mine_later = hold(mine_later)
    other_later = swap_cores(mine_later)
    acc_a, h, cx = call(
        k_first,
        [sums, tile, tile32],
        [mine, other, w, bias, cx, h, acc_a],
        aliases={4: 2, 5: 1, 6: 0},
        scratch=[pltpu.VMEM((2,) + PAIR, bf16)],
        part=0.3,
    )

    recv = swap_cores(h)
    acc_a, acc_b = call(
        k_second,
        [sums, sums],
        [mine_later, other_later, w, acc_a, acc_b],
        aliases={3: 0, 4: 1},
        scratch=[pltpu.VMEM(PAIR, bf16)],
        part=0.5,
    )
    mine = swap_rows(call(k_pick, [row], [h, recv])[0])
    acc_a, acc_b, cx, h2, s = call(
        k_third,
        [sums, sums, tile32, tile, stack],
        [h, recv, w, bias, cx, acc_a, acc_b],
        aliases={4: 2, 5: 0, 6: 1},
        part=0.25,
    )
    mine = hold(mine)
    other = swap_cores(mine)
    acc_a, acc_b = call(k_ends, [sums, sums], [w, s, acc_a, acc_b], aliases={2: 0, 3: 1}, part=0.2)
    acc_a, acc_b, cx, h = call(
        k_fourth,
        [sums, sums, tile32, tile],
        [mine, other, w, bias, cx, h2, acc_a, acc_b],
        aliases={4: 2, 5: 3, 6: 0, 7: 1},
        scratch=[pltpu.VMEM(PAIR, bf16)],
        part=0.2,
    )

    recv = swap_cores(h)
    acc_b, s = call(k_fifth, [sums, vm(CENTER, bf16)], [h, w, acc_b], aliases={2: 0}, part=0.22)
    mine = swap_rows(call(k_pick_two, [two_rows], [h, recv])[0], 1)
    hv, cv = vm((ROWS, COLS, CH), bf16), vm((ROWS, COLS, CH), f32)
    acc_b, s = call(k_sixth, [sums, vm(CENTER, bf16)], [recv, w, s, acc_b], aliases={3: 0}, part=0.45)
    acc_b, hid, cell = call(k_seventh, [sums, hv, cv], [h, cx, w, bias, s, acc_b], aliases={5: 0}, part=0.25)
    mine = hold(mine)
    other = swap_cores(mine)
    side = pltpu.VMEM((2, 3, COLS, CH), bf16)
    acc_b, hid, cell = call(
        k_mine,
        [sums, hv, cv],
        [mine, cx, w, bias, hid, cell, acc_b],
        aliases={4: 1, 5: 2, 6: 0},
        scratch=[side],
        part=0.2,
    )
    _, _, _, ho, co = call(
        k_last,
        [
            sums,
            hv,
            cv,
            jax.ShapeDtypeStruct((1, ROWS, COLS, CH), bf16),
            jax.ShapeDtypeStruct((1, ROWS, COLS, CH), f32),
        ],
        [other, cx, w, bias, hid, cell, acc_b],
        aliases={4: 1, 5: 2, 6: 0},
        far_out=(3, 4),
        scratch=[side, pltpu.SemaphoreType.DMA((2, ROWS))],
        part=0.2,
    )
    return ho, co


def solution(mesh):
    placed = (
        P(None, "gy", "gx", None),
        P("layer", "gy", "gx", None),
        P("layer", "gy", "gx", None),
        P("layer", None, None),
        P(),
    )
    return jax.shard_map(
        per_device,
        mesh=mesh,
        in_specs=placed,
        out_specs=(P("layer", "gy", "gx", None), P("layer", "gy", "gx", None)),
        check_vma=False,
    )
```
